256 devices in a mesh: angle: 2 (over z_hi), src: 16 (over x, z_lo), tile: 8 (over y, core).
Axes of the slice: x: 4, y: 4, z: 8 (z_hi: 2, z_lo: 4; z = z_hi * 4 + z_lo), core: 2. Of those that a mesh axis runs over, the one named last changes fastest.
Arguments:
- spectra: bfloat16 [32, 16, 2, 4096], P('tile', 'angle', None, 'src'), may hold values from -6 to 6
- cotangent: float32 [32, 128, 128], P('tile'), may hold values from -6 to 6
- pupil_field: bfloat16 [2048, 2, 4096], P(('angle', 'src', 'tile')), may hold values from -4 to 4
- source_grid: int32 [2048, 2], P(('angle', 'src')), may hold values from -8 to 8
- cutoff: int32 [2048], P(('angle', 'src')), may hold values from 256 to 784
- stencil: int32 [2048, 4], P(('angle', 'src')), may hold values from 0 to 15, as said below
- interp_weights: bfloat16 [2048, 4], P(('angle', 'src')), may hold values from 0.099609375 to 1
- source_weight: float32 [2048], P(('angle', 'src')), may hold values from 0.5 to 4
Outputs:
- grad_spectra: float32 [32, 16, 2, 4096], P('tile', 'angle', None, 'src')
The draws below stay inside these ranges and needn't reach their ends.
Inputs may be any that keep to these rules, and one draw needn't show every extreme that they name: `stencil`: the four entries of each source point are the corners c, c + 1, c + 4, c + 5 of one cell of the 16 reference angles laid out as a 4 x 4 grid (c = 4 i + j with i, j below 3).
All inputs are finite; a program needn't handle non-finite values.
Results may differ from the reference program's by a relative error of at most 0.0074.
Values may be sent and summed in bfloat16 or wider, within the bound.
A program may use at most 64 MiB of HBM per device.

```python
import math
import jax
import jax.numpy as jnp
from jax import lax

FQ = 64
NP = 128
ANGLES = 16
ORDERS = 4096
SRC = 2048
TILES = 32


def draw_stencil(key, part):
    key = jax.random.fold_in(key, 11)
    grid_side = math.isqrt(ANGLES)
    cells = jax.random.randint(key, (SRC, 2), 0, grid_side - 1)
    corner = cells[:, 0] * grid_side + cells[:, 1]
    return jnp.stack([corner, corner + 1, corner + grid_side, corner + grid_side + 1], axis=1).astype(jnp.int32)


def plant(values, rng, smallest, largest):
    extent = values.shape
    spot = [jax.random.randint(jax.random.fold_in(rng, axis), (), 0, extent[axis]) for axis in range(len(extent))]
    values = values.at[tuple(spot)].set(smallest)
    longest = extent.index(max(extent))
    spot[longest] = (spot[longest] + 1) % extent[longest]
    return values.at[tuple(spot)].set(largest)


def block_levels(rng, dims, shards, low, top_value):
    level = 1.0
    for axis_at, shards_of in shards:
        steps = jax.random.uniform(jax.random.fold_in(jax.random.fold_in(rng, 6), axis_at), (shards_of,), jnp.float32, low / len(shards), top_value / len(shards))
        level = level * jnp.repeat(jnp.exp(steps), dims[axis_at] // shards_of).reshape((-1,) + (1,) * (len(dims) - 1 - axis_at))
    return level


def normal_values(stream_key, extent, deviation, limit, cuts=(), kind=jnp.bfloat16):
    level = block_levels(stream_key, extent, cuts, -0.22, 0.18) if cuts else 1.0
    result = jax.random.normal(stream_key, extent, jnp.float32) * deviation * level
    return jnp.minimum(jnp.maximum(result, -limit), limit).astype(kind)


def setup_inputs(seed: int = 0) -> dict:
    key_of = jax.random.split(jax.random.key(seed), 9)
    return {
        "spectra": normal_values(key_of[0], (TILES, ANGLES, 2, ORDERS), 1.0, 6.0, ((0, 8), (1, 2), (3, 16))),
        "cotangent": normal_values(key_of[1], (TILES, NP, NP), 1.0, 6.0, ((0, 8),), jnp.float32),
        "pupil_field": normal_values(key_of[2], (SRC, 2, ORDERS), 0.7, 4.0, ((0, 256),)),
        "source_grid": plant(jax.random.randint(key_of[3], (SRC, 2), 0 - FQ // 8, FQ // 8 + 1), jax.random.fold_in(key_of[3], 1), 0 - FQ // 8, (FQ // 8 + 1) - 1).astype(jnp.int32),
        "cutoff": plant(jax.random.randint(key_of[4], (SRC,), FQ * FQ // 16, FQ * FQ * 49 // 256 + 1), jax.random.fold_in(key_of[4], 1), FQ * FQ // 16, (FQ * FQ * 49 // 256 + 1) - 1).astype(jnp.int32),
        "stencil": draw_stencil(jax.random.fold_in(key_of[8], 71), 0),
        "interp_weights": jnp.clip(0.099609375 + 0.9003906 * jax.random.uniform(key_of[6], (SRC, 4), jnp.float32) ** block_levels(key_of[6], (SRC, 4), ((0, 32),), -0.2, 0.2), 0.099609375, 1.0).astype(jnp.bfloat16),
        "source_weight": jnp.clip(jnp.exp(math.log(4.0) - 2.0794415 * jax.random.uniform(key_of[7], (SRC,), jnp.float32) ** block_levels(key_of[7], (SRC,), ((0, 32),), -0.2, 0.2)), 0.5, 4.0),
    }


highest = lax.Precision.HIGHEST

def dft_tables(side_orders, samples):
    frequency = jnp.arange(side_orders, dtype=jnp.int32) - side_orders // 2
    position = jnp.arange(samples, dtype=jnp.int32)
    residue = jnp.mod(position[:, None] * frequency[None, :], samples)
    phases = residue.astype(jnp.float32) * (2.0 * math.pi / samples)
    factor = 1.0 / math.sqrt(side_orders)
    cosine = jnp.cos(phases) * factor
    sine_table = jnp.sin(phases) * factor
    right_table = jnp.stack([jnp.stack([cosine.T, sine_table.T], axis=1), jnp.stack([-sine_table.T, cosine.T], axis=1)], axis=0)
    left_table = jnp.stack([jnp.stack([cosine, -sine_table], axis=1), jnp.stack([sine_table, cosine], axis=1)], axis=0)
    return (right_table.astype(jnp.bfloat16), left_table.astype(jnp.bfloat16))

def angle_weights(stencil, interp_weights, angle_count):
    labels = jnp.arange(angle_count, dtype=jnp.int32)
    matches = (stencil[:, :, None] == labels[None, None, :]).astype(jnp.float32)
    return lax.optimization_barrier(jnp.sum(matches * interp_weights.astype(jnp.float32)[:, :, None], axis=1)).astype(jnp.bfloat16)

def pupil_disc(source_grid, cutoff, side_orders):
    frequency = jnp.arange(side_orders, dtype=jnp.int32) - side_orders // 2
    along_first = frequency[None, :, None] + source_grid[:, 0][:, None, None]
    along_second = frequency[None, None, :] + source_grid[:, 1][:, None, None]
    within = along_first * along_first + along_second * along_second <= cutoff[:, None, None]
    return within.astype(jnp.float32).reshape(source_grid.shape[0], side_orders * side_orders)

def gradient_block(mixed, pupil_rows, disc, weight, cotangent, right_table, left_table):
    number = mixed.shape[0]
    tile_count = mixed.shape[1]
    side_orders = right_table.shape[1]
    pupil_real = pupil_rows[:, 0].astype(jnp.float32)[:, None, :]
    pupil_imag = pupil_rows[:, 1].astype(jnp.float32)[:, None, :]
    inside = disc[:, None, :]
    mixed_real = mixed[:, :, 0]
    mixed_imag = mixed[:, :, 1]
    field_real = inside * (pupil_real * mixed_real - pupil_imag * mixed_imag)
    field_imag = inside * (pupil_real * mixed_imag + pupil_imag * mixed_real)
    spectrum = jnp.stack([field_real, field_imag], axis=2).astype(jnp.bfloat16)
    spectrum = spectrum.reshape(number, tile_count, 2, side_orders, side_orders)
    right_wide = right_table.astype(jnp.float32)
    left_wide = left_table.astype(jnp.float32)
    halfway = jnp.einsum('btpyf,pfqx->btyqx', spectrum.astype(jnp.float32), right_wide, precision=highest).astype(jnp.bfloat16)
    image_field = jnp.einsum('ryqf,btfqx->btryx', left_wide, halfway.astype(jnp.float32), precision=highest)
    factor = weight[:, None, None, None] * cotangent[None]
    adjoint = (factor[:, :, None] * image_field).astype(jnp.bfloat16)
    back_half = jnp.einsum('btryx,rxqf->btyqf', adjoint.astype(jnp.float32), left_wide, precision=highest).astype(jnp.bfloat16)
    spectral = jnp.einsum('pfqy,btyqx->btpfx', right_wide, back_half.astype(jnp.float32), precision=highest)
    spectral = spectral.reshape(number, tile_count, 2, side_orders * side_orders)
    back_real = spectral[:, :, 0]
    back_imag = spectral[:, :, 1]
    grad_real = inside * (pupil_real * back_real + pupil_imag * back_imag)
    grad_imag = inside * (pupil_real * back_imag - pupil_imag * back_real)
    return jnp.stack([grad_real, grad_imag], axis=2)

def reference(spectra, cotangent, pupil_field, source_grid, cutoff, stencil, interp_weights, source_weight):
    right_table, left_table = dft_tables(FQ, NP)
    weights = angle_weights(stencil, interp_weights, ANGLES)
    disc = pupil_disc(source_grid, cutoff, FQ)
    scaled = source_weight * (2.0 / math.sqrt(SRC))
    spectra_wide = spectra.astype(jnp.float32)
    block_size = math.gcd(SRC, 8)
    rounds = SRC // block_size

    def accumulate(running, pieces):
        block_weights, block_pupil, block_disc, block_scaled = pieces
        wide_weights = block_weights.astype(jnp.float32)
        mixed = jnp.einsum('sk,tkpf->stpf', wide_weights, spectra_wide, precision=highest)
        gradient = gradient_block(mixed, block_pupil, block_disc, block_scaled, cotangent, right_table, left_table)
        added = jnp.einsum('sk,stpf->tkpf', wide_weights, gradient, precision=highest)
        return (running + added, None)
    pieces = (weights.reshape(rounds, block_size, ANGLES), pupil_field.reshape(rounds, block_size, 2, FQ * FQ), disc.reshape(rounds, block_size, FQ * FQ), scaled.reshape(rounds, block_size))
    initial = jnp.zeros((TILES, ANGLES, 2, FQ * FQ), jnp.float32)
    running, unused = lax.scan(accumulate, initial, pieces)
    return running
```

```python
import functools
import math

import jax
import jax.numpy as jnp
import ml_dtypes
import numpy as np
from jax import lax
from jax.experimental import pallas as pl
from jax.experimental.pallas import tpu as pltpu
from jax.sharding import PartitionSpec as P

FQ = 64
NP = 128
NX, NY, NZ = 4, 4, 8
BF = jnp.bfloat16
F32 = jnp.float32
MESH = pl.DeviceIdType.MESH


def dft_matrices():
    f = np.arange(FQ) - FQ // 2
    phase = np.mod(np.arange(NP)[:, None] * f[None, :], NP) * (2 * math.pi / NP)
    c, s = np.cos(phase) / math.sqrt(FQ), np.sin(phase) / math.sqrt(FQ)
    right = np.zeros((2, 2, 64, 2, 2, 128))
    left = np.zeros((2, 128, 2, 2, 32))
    for p in range(2):
        right[0, p, :, p, 0], right[0, p, :, p, 1] = c.T, s.T
        right[1, p, :, p, 0], right[1, p, :, p, 1] = -s.T, c.T
        left[0, :, p, 0], left[0, :, p, 1] = c[:, p::2], -s[:, p::2]
        left[1, :, p, 0], left[1, :, p, 1] = s[:, p::2], c[:, p::2]
    right, left = right.reshape(256, 512), left.reshape(256, 128)
    return [np.ascontiguousarray(v).astype(ml_dtypes.bfloat16) for v in (right, left, left.T, right.T)]


def dot(a, b):
    return jnp.dot(a, b, preferred_element_type=F32)


def columns_of(shape, dim):
    c = lax.broadcasted_iota(jnp.int32, shape, dim)
    x, z, k8, i2 = c >> 7, (c >> 4) & 7, (c >> 1) & 7, c & 1
    return (z >> 2) * 8 + k8, 2 * (x * 4 + (z & 3)) + i2


def source_block(n, e, spec, pupil, right, left, left_t, right_t, cot):
    mixed = dot(e, spec)
    mr, mi = mixed[:, :128], mixed[:, 128:]
    pr, pi = pupil[:, :128].astype(F32), pupil[:, 128:].astype(F32)
    field = jnp.concatenate([(pr * mr - pi * mi).astype(BF), (pr * mi + pi * mr).astype(BF)], axis=1)
    half = dot(field, right).astype(BF)
    wide = jnp.concatenate([cot, cot], axis=1)
    wide = jnp.concatenate([wide, wide], axis=0)
    rows = []
    for q in range(n // 2):
        pair = []
        for s in (2 * q, 2 * q + 1):
            pair.append(jnp.concatenate([half[s * 32 : s * 32 + 32, c * 128 : c * 128 + 128] for c in range(4)], axis=0))
        image = dot(left, jnp.concatenate(pair, axis=1))
        adjoint = (image * wide).astype(BF)
        back = dot(left_t, adjoint).astype(BF)
        for s in range(2):
            rows.append(jnp.concatenate([back[c * 32 : c * 32 + 32, s * 128 : s * 128 + 128] for c in range(4)], axis=1))
    spectrum = dot(jnp.concatenate(rows, axis=0), right_t)
    br, bi = spectrum[:, :128], spectrum[:, 128:]
    return jnp.concatenate([(pr * br + pi * bi).astype(BF), (pr * bi - pi * br).astype(BF)], axis=1)


def kernel(
    own_spec, own_pupil, cot, stencil, interp, weight, grid, cutoff, right, left, left_t, right_t,
    out,
    spec, pupil, mixrow, e, et, acc, send_x, recv_x, send_z, recv_z,
    zs_sem, zr_sem, xs_sem, xr_sem, ps_sem, pr_sem, cs_sem, cr_sem, rxs_sem, rxr_sem, rzs_sem, rzr_sem,
):
    angle, src, tile = lax.axis_index("angle"), lax.axis_index("src"), lax.axis_index("tile")
    x, z = src // 4, angle * 4 + lax.rem(src, 4)
    y, core = tile // 2, lax.rem(tile, 2)

    def at_x(d):
        return {"src": lax.rem(x + d, NX) * 4 + lax.rem(src, 4)}

    def at_z(d):
        w = lax.rem(z + d, NZ)
        return {"angle": w // 4, "src": x * 4 + lax.rem(w, 4)}

    def at_y(d):
        return {"tile": lax.rem(y + d, NY) * 2 + core}

    twin = {"tile": y * 2 + 1 - core}
    peers = [at_z(d) for d in range(1, NZ)] + [at_x(d) for d in range(1, NX)] + [at_y(d) for d in range(1, NY)] + [twin]
    barrier = pltpu.get_barrier_semaphore()
    for peer in peers:
        pl.semaphore_signal(barrier, inc=1, device_id=peer, device_id_type=MESH)
    pl.semaphore_wait(barrier, len(peers))

    def remote(src_ref, dst_ref, send, recv, peer):
        return pltpu.make_async_remote_copy(
            src_ref=src_ref, dst_ref=dst_ref, send_sem=send, recv_sem=recv, device_id=peer, device_id_type=MESH
        )

    zrows = pl.ds(pl.multiple_of(x * 128 + z * 16, 16), 16)
    xrows = pl.ds(pl.multiple_of(x * 128, 128), 128)

    def gather_z(t, d):
        rows = spec.at[t, zrows, :]
        return remote(own_spec.at[t], rows, zs_sem.at[t, d - 1], zr_sem.at[t, d - 1], at_z(d))

    def gather_x(t, d):
        rows = spec.at[t, xrows, :]
        return remote(rows, rows, xs_sem.at[t, d - 1], xr_sem.at[t, d - 1], at_x(d))

    for t in range(4):
        for d in range(1, NZ):
            gather_z(t, d).start()
    for t in range(4):
        spec[t, zrows, :] = own_spec[t]

    lane = lax.broadcasted_iota(jnp.int32, (32, 128), 1)
    fa = 2 * lax.broadcasted_iota(jnp.int32, (32, 128), 0) + (lane >> 6) - 32
    fb = (lane & 63) - 32

    def mask(s8, carry):
        s = tile * 8 + s8
        da, db = fa + grid[s, 0], fb + grid[s, 1]
        inside = da * da + db * db <= cutoff[s]
        inside = jnp.concatenate([inside, inside], axis=1)
        rows = pl.ds(pl.multiple_of(s * 32, 32), 32)
        value = own_pupil[pl.ds(pl.multiple_of(s8 * 32, 32), 32), :].astype(F32)
        pupil[rows, :] = jnp.where(inside, value, 0.0).astype(BF)
        return carry

    lax.fori_loop(0, 8, mask, 0)

    def pupil_rows(yy):
        return pupil.at[pl.ds(pl.multiple_of((yy * 2 + core) * 256, 256), 256), :]

    def pupil_y(d):
        return remote(pupil_rows(y), pupil_rows(y), ps_sem.at[d - 1], pr_sem.at[d - 1], at_y(d))

    def pupil_core(j):
        rows = pupil_rows(lax.rem(y + j, NY))
        return remote(rows, rows, cs_sem.at[j], cr_sem.at[j], twin)

    for d in range(1, NY):
        pupil_y(d).start()
    pupil_core(0).start()

    ks, _ = columns_of((64, 512), 1)
    mix = jnp.zeros((64, 512), F32)
    for j in range(4):
        mix += jnp.where(stencil[:, j : j + 1] == ks, interp[:, j : j + 1].astype(F32), 0.0)
    mixrow[...] = mix
    _, i_row = columns_of((32, 512), 1)
    diagonal = (lax.broadcasted_iota(jnp.int32, (32, 512), 0) == i_row).astype(F32)

    def fill_e(s, carry):
        row = mixrow[pl.ds(s, 1), :]
        e[pl.ds(pl.multiple_of(s * 32, 32), 32), :] = (row * diagonal).astype(BF)
        return carry

    lax.fori_loop(0, 64, fill_e, 0)
    scaled = (mix * (weight[...] * (2.0 / math.sqrt(2048)))).T.astype(BF)
    _, i_col = columns_of((512, 512), 0)
    spread = lax.broadcasted_iota(jnp.int32, (512, 512), 1)
    hit = (spread & 31) == i_col
    source_of = lax.broadcasted_iota(jnp.int32, (64, 512), 1) >> 5
    source_at = lax.broadcasted_iota(jnp.int32, (64, 512), 0)
    for yy in range(4):
        pick = (source_of + yy * 16 == source_at).astype(BF)
        et[yy] = jnp.where(hit, dot(scaled, pick), 0.0).astype(BF)

    for t in range(4):
        for d in range(1, NZ):
            gather_z(t, d).wait_recv()
        for d in range(1, NX):
            gather_x(t, d).start()

    def reduce_x(t, d):
        to = lax.rem(x + d, NX)
        rows = send_x.at[t, pl.ds(pl.multiple_of(to * 128, 128), 128), :]
        return remote(rows, recv_x.at[t, d - 1], rxs_sem.at[t, d - 1], rxr_sem.at[t, d - 1], at_x(d))

    def reduce_z(t, d):
        to = lax.rem(z + d, NZ)
        rows = send_z.at[t, pl.ds(pl.multiple_of(to * 16, 16), 16), :]
        return remote(rows, recv_z.at[t, d - 1], rzs_sem.at[t, d - 1], rzr_sem.at[t, d - 1], at_z(d))

    def turn_x(t):
        total = send_x[t, xrows, :].astype(F32)
        for d in range(1, NX):
            reduce_x(t, d).wait_recv()
        for d in range(1, NX):
            total += recv_x[t, d - 1].astype(F32)
        send_z[t] = total.astype(BF)
        for d in range(1, NZ):
            reduce_z(t, d).start()

    def turn_z(t):
        total = send_z[t, pl.ds(pl.multiple_of(z * 16, 16), 16), :].astype(F32)
        for d in range(1, NZ):
            reduce_z(t, d).wait_recv()
        for d in range(1, NZ):
            total += recv_z[t, d - 1].astype(F32)
        out[t] = total

    def one_tile(t, carry):
        for d in range(1, NX):
            gather_x(t, d).wait_recv()

        def one_block(j, inner):
            yy = lax.rem(y + j, NY)

            @pl.when(t == 0)
            def _():
                @pl.when(j > 0)
                def _():
                    pltpu.make_async_remote_copy(
                        src_ref=pupil_rows(yy), dst_ref=pupil_rows(yy), send_sem=ps_sem.at[0],
                        recv_sem=pr_sem.at[NY - 1 - j], device_id=twin, device_id_type=MESH,
                    ).wait_recv()
                    pupil_core(j).start()

                pupil_core(j).wait_recv()

            rows = pl.ds(pl.multiple_of(yy * 512, 512), 512)
            grad = source_block(
                16, e[rows, :], spec[t], pupil[rows, :], right[...], left[...], left_t[...], right_t[...], cot[t]
            )
            added = dot(et[yy], grad)

            @pl.when(j == 0)
            def _():
                acc[...] = added

            @pl.when(j > 0)
            def _():
                acc[...] += added

            @pl.when(jnp.logical_and(t > 0, j == 0))
            def _():
                turn_x(t - 1)

            @pl.when(jnp.logical_and(t > 0, j == 1))
            def _():
                turn_z(t - 1)

            return inner

        lax.fori_loop(0, NY, one_block, 0)
        send_x[t] = acc[...].astype(BF)
        for d in range(1, NX):
            reduce_x(t, d).start()
        return carry

    lax.fori_loop(0, 4, one_tile, 0)
    turn_x(3)
    turn_z(3)

    for t in range(4):
        for d in range(1, NZ):
            gather_z(t, d).wait_send()
            reduce_z(t, d).wait_send()
        for d in range(1, NX):
            gather_x(t, d).wait_send()
            reduce_x(t, d).wait_send()
    for d in range(1, NY):
        pupil_y(d).wait_send()
    for j in range(NY):
        pupil_core(j).wait_send()


def shards(spectra, cotangent, pupil_field, source_grid, cutoff, stencil, interp_weights, source_weight):
    own_spec = spectra.reshape(4, 8, 2, 2, 128).transpose(0, 1, 3, 2, 4).reshape(4, 16, 256)
    own_pupil = pupil_field.reshape(8, 2, 32, 128).transpose(0, 2, 1, 3).reshape(256, 256)
    vmem = pl.BlockSpec(memory_space=pltpu.VMEM)
    smem = pl.BlockSpec(memory_space=pltpu.SMEM)
    dma = pltpu.SemaphoreType.DMA
    result = pl.pallas_call(
        kernel,
        out_shape=jax.ShapeDtypeStruct((4, 16, 256), F32),
        in_specs=[vmem] * 6 + [smem] * 2 + [vmem] * 4,
        out_specs=vmem,
        scratch_shapes=[
            pltpu.VMEM((4, 512, 256), BF),
            pltpu.VMEM((2048, 256), BF),
            pltpu.VMEM((64, 512), F32),
            pltpu.VMEM((2048, 512), BF),
            pltpu.VMEM((4, 512, 512), BF),
            pltpu.VMEM((512, 256), F32),
            pltpu.VMEM((4, 512, 256), BF),
            pltpu.VMEM((4, 3, 128, 256), BF),
            pltpu.VMEM((4, 128, 256), BF),
            pltpu.VMEM((4, 7, 16, 256), BF),
            dma((4, 7)), dma((4, 7)), dma((4, 3)), dma((4, 3)),
            dma((3,)), dma((3,)), dma((4,)), dma((4,)),
            dma((4, 3)), dma((4, 3)), dma((4, 7)), dma((4, 7)),
        ],
        compiler_params=pltpu.CompilerParams(
            collective_id=0, has_side_effects=True, vmem_limit_bytes=56 << 20
        ),
    )(
        own_spec, own_pupil, cotangent, stencil, interp_weights, source_weight.reshape(64, 1), source_grid, cutoff,
        *[jnp.asarray(v) for v in dft_matrices()],
    )
    return result.reshape(4, 8, 2, 2, 128).transpose(0, 1, 3, 2, 4).reshape(4, 8, 2, 256)


def solution(mesh):
    placed = (
        P("tile", "angle", None, "src"),
        P("tile", None, None),
        P(("angle", "src", "tile"), None, None),
        P(("angle", "src"), None),
        P(("angle", "src")),
        P(("angle", "src"), None),
        P(("angle", "src"), None),
        P(("angle", "src")),
    )
    return jax.shard_map(
        shards, mesh=mesh, in_specs=placed, out_specs=P("tile", "angle", None, "src"), check_vma=False
    )
```

```python
import functools
import math

import jax
import jax.numpy as jnp
import ml_dtypes
import numpy as np
from jax import lax
from jax.experimental import pallas as pl
from jax.experimental.pallas import tpu as pltpu
from jax.sharding import PartitionSpec as P

FQ = 64
NP = 128
NX, NY, NZ = 4, 4, 8
BF = jnp.bfloat16
F32 = jnp.float32
MESH = pl.DeviceIdType.MESH


def dft_matrices():
    f = np.arange(FQ) - FQ // 2
    phase = np.mod(np.arange(NP)[:, None] * f[None, :], NP) * (2 * math.pi / NP)
    c, s = np.cos(phase) / math.sqrt(FQ), np.sin(phase) / math.sqrt(FQ)
    right = np.zeros((2, 2, 64, 2, 2, 128))
    left = np.zeros((2, 128, 2, 2, 32))
    for p in range(2):
        right[0, p, :, p, 0], right[0, p, :, p, 1] = c.T, s.T
        right[1, p, :, p, 0], right[1, p, :, p, 1] = -s.T, c.T
        left[0, :, p, 0], left[0, :, p, 1] = c[:, p::2], -s[:, p::2]
        left[1, :, p, 0], left[1, :, p, 1] = s[:, p::2], c[:, p::2]
    right, left = right.reshape(256, 512), left.reshape(256, 128)
    return [np.ascontiguousarray(v).astype(ml_dtypes.bfloat16) for v in (right, left, left.T, right.T)]


def dot(a, b):
    return jnp.dot(a, b, preferred_element_type=F32)


def join(values, axis):
    return jnp.concatenate(values, axis=axis)


def source_block(n, h, e, spec, pupil, right, left, left_t, right_t, cot):
    m = n // h
    mixed = [dot(e, spec[x * 128 : x * 128 + 128]) for x in range(NX)]
    pupils, halves = [], []
    for g in range(h):
        p = pupil[g * m * 32 : (g + 1) * m * 32]
        pr, pi = p[:, :128].astype(F32), p[:, 128:].astype(F32)
        pupils.append((pr, pi))
        own = join([mixed[x][s * 8 : s * 8 + 8] for s in range(g * m, (g + 1) * m) for x in range(NX)], 0)
        mr, mi = own[:, :128], own[:, 128:]
        halves.append(join([(pr * mr - pi * mi).astype(BF), (pr * mi + pi * mr).astype(BF)], 1))
    halves = [dot(field, right).astype(BF) for field in halves]
    wide = join([cot, cot], 1)
    wide = join([wide, wide], 0)
    adjoints = []
    for q in range(n // 2):
        pair = []
        for s in (2 * q, 2 * q + 1):
            half, row = halves[s // m], s % m * 32
            pair.append(join([half[row : row + 32, c * 128 : c * 128 + 128] for c in range(4)], 0))
        adjoints.append((dot(left, join(pair, 1)) * wide).astype(BF))
    backs = [dot(left_t, adjoint).astype(BF) for adjoint in adjoints]
    rows = []
    for back in backs:
        for s in range(2):
            rows.append(join([back[c * 32 : c * 32 + 32, s * 128 : s * 128 + 128] for c in range(4)], 1))
    spectra = [dot(join(rows[g * m : (g + 1) * m], 0), right_t) for g in range(h)]
    grads = []
    for (pr, pi), spectrum in zip(pupils, spectra):
        br, bi = spectrum[:, :128], spectrum[:, 128:]
        grads.append(join([pr * br + pi * bi, pr * bi - pi * br], 1))
    return [
        join([grads[s // m][s % m * 32 + x * 8 : s % m * 32 + x * 8 + 8] for s in range(n)], 0).astype(BF)
        for x in range(NX)
    ]


def kernel(
    raw_spec, raw_pupil, cot, stencil, interp, weight, grid, cutoff, right, left, left_t, right_t,
    out,
    own_spec, spec, pupil, e, et, acc, send_x, recv_x, send_z, recv_z,
    zs_sem, zr_sem, xs_sem, xr_sem, ps_sem, pr_sem, cs_sem, cr_sem, rxs_sem, rxr_sem, rzs_sem, rzr_sem,
):
    angle, src, tile = lax.axis_index("angle"), lax.axis_index("src"), lax.axis_index("tile")
    x, z = src // 4, angle * 4 + lax.rem(src, 4)
    y, core = tile // 2, lax.rem(tile, 2)

    def at_x(d):
        return {"src": lax.rem(x + d, NX) * 4 + lax.rem(src, 4)}

    def at_z(d):
        w = lax.rem(z + d, NZ)
        return {"angle": w // 4, "src": x * 4 + lax.rem(w, 4)}

    def at_y(d):
        return {"tile": lax.rem(y + d, NY) * 2 + core}

    twin = {"tile": y * 2 + 1 - core}
    peers = [at_z(d) for d in (4, 3, 5, 2, 6, 1, 7)] + [at_x(d) for d in (2, 1, 3)] + [at_y(d) for d in (2, 1, 3)] + [twin]
    barrier = pltpu.get_barrier_semaphore()
    for peer in peers:
        pl.semaphore_signal(barrier, inc=1, device_id=peer, device_id_type=MESH)

    for t in range(4):
        part = raw_spec[t * 16 : t * 16 + 16]
        own_spec[t] = join([part[:, 0], part[:, 1]], 1)

    lane = lax.broadcasted_iota(jnp.int32, (32, 128), 1)
    fa = 2 * lax.broadcasted_iota(jnp.int32, (32, 128), 0) + (lane >> 6) - 32
    fb = (lane & 63) - 32

    def mask(s8, carry):
        s = tile * 8 + s8
        da, db = fa + grid[0, s], fb + grid[1, s]
        inside = da * da + db * db <= cutoff[s]
        inside = join([inside, inside], 1)
        part = raw_pupil[pl.ds(pl.multiple_of(s8 * 32, 32), 32)]
        value = join([part[:, 0], part[:, 1]], 1).astype(F32)
        pupil[pl.ds(pl.multiple_of(s * 32, 32), 32), :] = jnp.where(inside, value, 0.0).astype(BF)
        return carry

    lax.fori_loop(0, 8, mask, 0)

    c = lax.broadcasted_iota(jnp.int32, (128, 64), 0)
    k_of = (c >> 6) * 8 + ((c >> 1) & 7)
    mix = jnp.zeros((128, 64), F32)
    for j in range(4):
        mix += jnp.where(stencil[j : j + 1, :] == k_of, interp[j : j + 1, :].astype(F32), 0.0)
    scaled = (mix * (weight[...] * (2.0 / math.sqrt(2048)))).astype(BF)
    mix = mix.astype(BF)
    c = lax.broadcasted_iota(jnp.int32, (128, 256), 0)
    col = lax.broadcasted_iota(jnp.int32, (128, 256), 1)
    hit = (col & 7) == ((c >> 4) & 3) * 2 + (c & 1)
    source_at = lax.broadcasted_iota(jnp.int32, (64, 256), 0)
    source_of = lax.broadcasted_iota(jnp.int32, (64, 256), 1) >> 3
    for k in range(2):
        pick = (source_of + k * 32 == source_at).astype(BF)
        et[k] = jnp.where(hit, dot(scaled, pick), 0.0).astype(BF)
        e[k] = jnp.where(hit, dot(mix, pick), 0.0).T.astype(BF)

    pl.semaphore_wait(barrier, len(peers))

    def remote(src_ref, dst_ref, send, recv, peer):
        return pltpu.make_async_remote_copy(
            src_ref=src_ref, dst_ref=dst_ref, send_sem=send, recv_sem=recv, device_id=peer, device_id_type=MESH
        )

    zrows = pl.ds(pl.multiple_of(x * 128 + z * 16, 16), 16)
    xrows = pl.ds(pl.multiple_of(x * 128, 128), 128)

    def gather_z(t, d):
        return remote(own_spec.at[t], spec.at[t, zrows, :], zs_sem.at[t, d - 1], zr_sem.at[t, d - 1], at_z(d))

    def gather_x(t, d):
        rows = spec.at[t, xrows, :]
        return remote(rows, rows, xs_sem.at[t, d - 1], xr_sem.at[t, d - 1], at_x(d))

    def pupil_rows(yy):
        return pupil.at[pl.ds(pl.multiple_of((yy * 2 + core) * 256, 256), 256), :]

    def pupil_y(d):
        return remote(pupil_rows(y), pupil_rows(y), ps_sem.at[d - 1], pr_sem.at[d - 1], at_y(d))

    def pupil_core(j):
        rows = pupil_rows(lax.rem(y + j, NY))
        return remote(rows, rows, cs_sem.at[j], cr_sem.at[j], twin)

    for t in range(4):
        for d in (4, 3, 5, 2, 6, 1, 7):
            gather_z(t, d).start()
        if t == 0:
            for d in range(1, NY):
                pupil_y(d).start()
            pupil_core(0).start()
    for t in range(4):
        spec[t, zrows, :] = own_spec[t]

    for t in range(4):
        for d in range(1, NZ):
            gather_z(t, d).wait_recv()
        for d in (2, 1, 3):
            gather_x(t, d).start()
        if t == 0:
            for d in range(1, NY):
                pupil_y(d).wait_recv()
                pupil_core(NY - d).start()

    def reduce_x(t, d):
        to = lax.rem(x + d, NX)
        rows = send_x.at[t, pl.ds(pl.multiple_of(to * 128, 128), 128), :]
        return remote(rows, recv_x.at[t, d - 1], rxs_sem.at[t, d - 1], rxr_sem.at[t, d - 1], at_x(d))

    def reduce_z(t, d):
        to = lax.rem(z + d, NZ)
        rows = send_z.at[t, pl.ds(pl.multiple_of(to * 16, 16), 16), :]
        return remote(rows, recv_z.at[t, d - 1], rzs_sem.at[t, d - 1], rzr_sem.at[t, d - 1], at_z(d))

    def turn_x(t):
        total = send_x[t, xrows, :].astype(F32)
        for d in range(1, NX):
            reduce_x(t, d).wait_recv()
        for d in range(1, NX):
            total += recv_x[t, d - 1].astype(F32)
        send_z[t] = total.astype(BF)
        for d in (4, 3, 5, 2, 6, 1, 7):
            reduce_z(t, d).start()

    def turn_z(t):
        total = send_z[t, pl.ds(pl.multiple_of(z * 16, 16), 16), :].astype(F32)
        for d in range(1, NZ):
            reduce_z(t, d).wait_recv()
        for d in range(1, NZ):
            total += recv_z[t, d - 1].astype(F32)
        out[t] = total

    def one_block(b, carry):
        t, k = b // 2, lax.rem(b, 2)

        @pl.when(k == 0)
        def _():
            for d in range(1, NX):
                gather_x(t, d).wait_recv()

        @pl.when(b == 0)
        def _():
            for j in range(NY):
                pupil_core(j).wait_recv()

        rows = pl.ds(pl.multiple_of(k * 1024, 1024), 1024)
        grads = source_block(
            32, 4, e[k], spec[t], pupil[rows, :], right[...], left[...], left_t[...], right_t[...], cot[t]
        )
        added = [dot(et[k], g) for g in grads]

        @pl.when(k == 0)
        def _():
            for i in range(NX):
                acc[i * 128 : i * 128 + 128, :] = added[i]

        @pl.when(k == 1)
        def _():
            for i in range(NX):
                send_x[t, i * 128 : i * 128 + 128, :] = (acc[i * 128 : i * 128 + 128, :] + added[i]).astype(BF)
            for d in (2, 1, 3):
                reduce_x(t, d).start()

        @pl.when(b == 4)
        def _():
            turn_x(0)

        @pl.when(b == 6)
        def _():
            turn_x(1)

        return carry

    lax.fori_loop(0, 8, one_block, 0)
    turn_x(2)
    turn_x(3)
    for t in range(4):
        turn_z(t)

    for t in range(4):
        for d in range(1, NZ):
            gather_z(t, d).wait_send()
            reduce_z(t, d).wait_send()
        for d in range(1, NX):
            gather_x(t, d).wait_send()
            reduce_x(t, d).wait_send()
    for d in range(1, NY):
        pupil_y(d).wait_send()
    for j in range(NY):
        pupil_core(j).wait_send()


def shards(spectra, cotangent, pupil_field, source_grid, cutoff, stencil, interp_weights, source_weight):
    own_spec = spectra.reshape(4, 8, 2, 2, 128).transpose(0, 1, 3, 2, 4).reshape(64, 2, 128)
    own_pupil = pupil_field.reshape(8, 2, 32, 128).transpose(0, 2, 1, 3).reshape(256, 2, 128)
    vmem = pl.BlockSpec(memory_space=pltpu.VMEM)
    smem = pl.BlockSpec(memory_space=pltpu.SMEM)
    dma = pltpu.SemaphoreType.DMA
    result = pl.pallas_call(
        kernel,
        out_shape=jax.ShapeDtypeStruct((4, 16, 256), F32),
        in_specs=[vmem] * 6 + [smem] * 2 + [vmem] * 4,
        out_specs=vmem,
        scratch_shapes=[
            pltpu.VMEM((4, 16, 256), BF),
            pltpu.VMEM((4, 512, 256), BF),
            pltpu.VMEM((2048, 256), BF),
            pltpu.VMEM((2, 256, 128), BF),
            pltpu.VMEM((2, 128, 256), BF),
            pltpu.VMEM((512, 256), F32),
            pltpu.VMEM((4, 512, 256), BF),
            pltpu.VMEM((4, 3, 128, 256), BF),
            pltpu.VMEM((4, 128, 256), BF),
            pltpu.VMEM((4, 7, 16, 256), BF),
            dma((4, 7)), dma((4, 7)), dma((4, 3)), dma((4, 3)),
            dma((3,)), dma((3,)), dma((4,)), dma((4,)),
            dma((4, 3)), dma((4, 3)), dma((4, 7)), dma((4, 7)),
        ],
        compiler_params=pltpu.CompilerParams(
            collective_id=0, has_side_effects=True, vmem_limit_bytes=56 << 20
        ),
    )(
        own_spec, own_pupil, cotangent, stencil.T, interp_weights.T, source_weight.reshape(1, 64), source_grid.T, cutoff,
        *[jnp.asarray(v) for v in dft_matrices()],
    )
    return result.reshape(4, 8, 2, 2, 128).transpose(0, 1, 3, 2, 4).reshape(4, 8, 2, 256)


def solution(mesh):
    placed = (
        P("tile", "angle", None, "src"),
        P("tile", None, None),
        P(("angle", "src", "tile"), None, None),
        P(("angle", "src"), None),
        P(("angle", "src")),
        P(("angle", "src"), None),
        P(("angle", "src"), None),
        P(("angle", "src")),
    )
    return jax.shard_map(
        shards, mesh=mesh, in_specs=placed, out_specs=P("tile", "angle", None, "src"), check_vma=False
    )
```

```python
import functools
import math

import jax
import jax.numpy as jnp
import ml_dtypes
import numpy as np
from jax import lax
from jax.experimental import pallas as pl
from jax.experimental.pallas import tpu as pltpu
from jax.sharding import PartitionSpec as P

FQ = 64
NP = 128
NX, NY, NZ = 4, 4, 8
BF = jnp.bfloat16
F32 = jnp.float32
MESH = pl.DeviceIdType.MESH
FAR_FIRST = (4, 3, 5, 2, 6, 1, 7)


def dft_matrices():
    f = np.arange(FQ) - FQ // 2
    phase = np.mod(np.arange(NP)[:, None] * f[None, :], NP) * (2 * math.pi / NP)
    c, s = np.cos(phase) / math.sqrt(FQ), np.sin(phase) / math.sqrt(FQ)
    right = np.zeros((2, 2, 64, 2, 2, 128))
    left = np.zeros((2, 128, 2, 2, 32))
    for p in range(2):
        right[0, p, :, p, 0], right[0, p, :, p, 1] = c.T, s.T
        right[1, p, :, p, 0], right[1, p, :, p, 1] = -s.T, c.T
        left[0, :, p, 0], left[0, :, p, 1] = c[:, p::2], -s[:, p::2]
        left[1, :, p, 0], left[1, :, p, 1] = s[:, p::2], c[:, p::2]
    right, left = right.reshape(256, 512), left.reshape(256, 128)
    return [np.ascontiguousarray(v).astype(ml_dtypes.bfloat16) for v in (right, left, left.T, right.T)]


def dot(a, b):
    return jnp.dot(a, b, preferred_element_type=F32)


def join(values, axis):
    return jnp.concatenate(values, axis=axis)


def source_block(n, h, e, spec, pupil, right, left, left_t, right_t, cot):
    m = n // h
    mixed = [dot(e, spec[x * 128 : x * 128 + 128]) for x in range(NX)]
    pupils, halves = [], []
    for g in range(h):
        p = pupil[g * m * 32 : (g + 1) * m * 32]
        pr, pi = p[:, :128].astype(F32), p[:, 128:].astype(F32)
        pupils.append((pr, pi))
        own = join([mixed[x][s * 8 : s * 8 + 8] for s in range(g * m, (g + 1) * m) for x in range(NX)], 0)
        mr, mi = own[:, :128], own[:, 128:]
        halves.append(join([(pr * mr - pi * mi).astype(BF), (pr * mi + pi * mr).astype(BF)], 1))
    halves = [dot(field, right).astype(BF) for field in halves]
    wide = join([cot, cot], 1)
    wide = join([wide, wide], 0)
    adjoints = []
    for q in range(n // 2):
        pair = []
        for s in (2 * q, 2 * q + 1):
            half, row = halves[s // m], s % m * 32
            pair.append(join([half[row : row + 32, c * 128 : c * 128 + 128] for c in range(4)], 0))
        adjoints.append((dot(left, join(pair, 1)) * wide).astype(BF))
    backs = [dot(left_t, adjoint).astype(BF) for adjoint in adjoints]
    rows = []
    for back in backs:
        for s in range(2):
            rows.append(join([back[c * 32 : c * 32 + 32, s * 128 : s * 128 + 128] for c in range(4)], 1))
    spectra = [dot(join(rows[g * m : (g + 1) * m], 0), right_t) for g in range(h)]
    grads = []
    for (pr, pi), spectrum in zip(pupils, spectra):
        br, bi = spectrum[:, :128], spectrum[:, 128:]
        grads.append(join([pr * br + pi * bi, pr * bi - pi * br], 1))
    return [
        join([grads[s // m][s % m * 32 + x * 8 : s % m * 32 + x * 8 + 8] for s in range(n)], 0).astype(BF)
        for x in range(NX)
    ]


def kernel(
    spec_hbm, pupil_hbm, cot_hbm, stencil_hbm, interp_hbm, weight_hbm, grid_hbm, cutoff_hbm,
    right_hbm, left_hbm, left_t_hbm, right_t_hbm,
    out,
    raw_spec, raw_pupil, cot, stencil, interp, weight, grid, cutoff, right, left, left_t, right_t,
    own_spec, spec, pupil, e, et, acc, send_x, recv_x, send_z, recv_z,
    in_sem, hello, zs_sem, zr_sem, xs_sem, xr_sem, ps_sem, pr_sem, cs_sem, cr_sem, rxs_sem, rxr_sem, rzs_sem, rzr_sem,
):
    angle, src, tile = lax.axis_index("angle"), lax.axis_index("src"), lax.axis_index("tile")
    x, z = src // 4, angle * 4 + lax.rem(src, 4)
    y, core = tile // 2, lax.rem(tile, 2)

    def at_x(d):
        return {"src": lax.rem(x + d, NX) * 4 + lax.rem(src, 4)}

    def at_z(d):
        w = lax.rem(z + d, NZ)
        return {"angle": w // 4, "src": x * 4 + lax.rem(w, 4)}

    def at_y(d):
        return {"tile": lax.rem(y + d, NY) * 2 + core}

    twin = {"tile": y * 2 + 1 - core}
    peers = [at_z(d) for d in FAR_FIRST] + [at_x(d) for d in (2, 1, 3)] + [at_y(d) for d in (2, 1, 3)]
    barrier = pltpu.get_barrier_semaphore()
    for peer in peers:
        pl.semaphore_signal(barrier, inc=1, device_id=peer, device_id_type=MESH)

    @pl.when(core == 0)
    def _():
        pl.semaphore_signal(barrier, inc=1, device_id=twin, device_id_type=MESH)

    pairs = [
        (spec_hbm, raw_spec), (grid_hbm, grid), (cutoff_hbm, cutoff), (pupil_hbm, raw_pupil), (stencil_hbm, stencil),
        (interp_hbm, interp), (weight_hbm, weight), (right_hbm, right), (left_hbm, left), (cot_hbm, cot),
        (left_t_hbm, left_t), (right_t_hbm, right_t),
    ]
    loads = [pltpu.make_async_copy(a, b, in_sem.at[i]) for i, (a, b) in enumerate(pairs)]
    for load in loads:
        load.start()

    loads[0].wait()
    for t in range(4):
        part = raw_spec[t * 16 : t * 16 + 16]
        own_spec[t] = join([part[:, 0], part[:, 1]], 1)

    for load in loads[1:4]:
        load.wait()
    lane = lax.broadcasted_iota(jnp.int32, (32, 128), 1)
    fa = 2 * lax.broadcasted_iota(jnp.int32, (32, 128), 0) + (lane >> 6) - 32
    fb = (lane & 63) - 32

    def pupil_rows(yy):
        return pl.ds(pl.multiple_of((core * 4 + yy) * 256, 256), 256)

    def mask(s8, carry):
        s = tile * 8 + s8
        da, db = fa + grid[0, s], fb + grid[1, s]
        inside = da * da + db * db <= cutoff[s]
        inside = join([inside, inside], 1)
        part = raw_pupil[pl.ds(pl.multiple_of(s8 * 32, 32), 32)]
        value = join([part[:, 0], part[:, 1]], 1).astype(F32)
        rows = pl.ds(pl.multiple_of((core * 4 + y) * 256 + s8 * 32, 32), 32)
        pupil[rows, :] = jnp.where(inside, value, 0.0).astype(BF)
        return carry

    lax.fori_loop(0, 8, mask, 0)

    for load in loads[4:7]:
        load.wait()
    c = lax.broadcasted_iota(jnp.int32, (128, 64), 0)
    k_of = (c >> 6) * 8 + ((c >> 1) & 7)
    mix = jnp.zeros((128, 64), F32)
    for j in range(4):
        mix += jnp.where(stencil[j : j + 1, :] == k_of, interp[j : j + 1, :].astype(F32), 0.0)
    scaled = (mix * (weight[...] * (2.0 / math.sqrt(2048)))).astype(BF)
    mix = mix.astype(BF)
    c = lax.broadcasted_iota(jnp.int32, (128, 256), 0)
    col = lax.broadcasted_iota(jnp.int32, (128, 256), 1)
    hit = (col & 7) == ((c >> 4) & 3) * 2 + (c & 1)
    source_at = lax.broadcasted_iota(jnp.int32, (64, 256), 0)
    col = lax.broadcasted_iota(jnp.int32, (64, 256), 1)
    source_of = (col >> 6) * 16 + ((col >> 3) & 7)
    for k in range(2):
        pick = (source_of + k * 8 == source_at).astype(BF)
        et[k] = jnp.where(hit, dot(scaled, pick), 0.0).astype(BF)
        e[k] = jnp.where(hit, dot(mix, pick), 0.0).T.astype(BF)

    pl.semaphore_wait(barrier, len(peers) + core)

    @pl.when(core == 1)
    def _():
        pl.semaphore_signal(hello, inc=1, device_id=twin, device_id_type=MESH)

    def remote(src_ref, dst_ref, send, recv, peer):
        return pltpu.make_async_remote_copy(
            src_ref=src_ref, dst_ref=dst_ref, send_sem=send, recv_sem=recv, device_id=peer, device_id_type=MESH
        )

    zrows = pl.ds(pl.multiple_of(x * 128 + z * 16, 16), 16)
    xrows = pl.ds(pl.multiple_of(x * 128, 128), 128)

    def gather_z(t, d):
        return remote(own_spec.at[t], spec.at[t, zrows, :], zs_sem.at[t, d - 1], zr_sem.at[t, d - 1], at_z(d))

    def gather_x(t, d):
        rows = spec.at[t, xrows, :]
        return remote(rows, rows, xs_sem.at[t, d - 1], xr_sem.at[t, d - 1], at_x(d))

    def pupil_y(d):
        rows = pupil.at[pupil_rows(y), :]
        return remote(rows, rows, ps_sem.at[d - 1], pr_sem.at[d - 1], at_y(d))

    def pupil_core(j):
        rows = pupil.at[pupil_rows(lax.rem(y + j, NY)), :]
        return remote(rows, rows, cs_sem.at[j], cr_sem.at[j], twin)

    for t in range(4):
        for d in FAR_FIRST:
            gather_z(t, d).start()
        if t == 0:
            for d in (2, 1, 3):
                pupil_y(d).start()
    for t in range(4):
        spec[t, zrows, :] = own_spec[t]
    for load in loads[7:]:
        load.wait()

    for t in range(4):
        for d in range(1, NZ):
            gather_z(t, d).wait_recv()
        for d in (2, 1, 3):
            gather_x(t, d).start()

    @pl.when(core == 0)
    def _():
        pl.semaphore_wait(hello, 1)

    pupil_core(0).start()
    for d in range(1, NY):
        pupil_y(d).wait_recv()
        pupil_core(NY - d).start()

    def reduce_x(t, d):
        to = lax.rem(x + d, NX)
        rows = send_x.at[t, pl.ds(pl.multiple_of(to * 128, 128), 128), :]
        return remote(rows, recv_x.at[t, d - 1], rxs_sem.at[t, d - 1], rxr_sem.at[t, d - 1], at_x(d))

    def z_block(d):
        return lax.rem(z + d, NZ) * 16

    def reduce_z(t, d):
        rows = send_z.at[t, pl.ds(pl.multiple_of(z_block(d), 16), 16), :]
        return remote(rows, recv_z.at[t, d - 1], rzs_sem.at[t, d - 1], rzr_sem.at[t, d - 1], at_z(d))

    def turn_x(t):
        for d in range(1, NX):
            reduce_x(t, d).wait_recv()
        for d in FAR_FIRST + (0,):
            rows = pl.ds(pl.multiple_of(z_block(d), 16), 16)
            total = send_x[t, pl.ds(pl.multiple_of(x * 128 + z_block(d), 16), 16), :].astype(F32)
            for w in range(NX - 1):
                total += recv_x[t, w, rows, :].astype(F32)
            send_z[t, rows, :] = total.astype(BF)
            if d:
                reduce_z(t, d).start()

    def turn_z(t):
        total = send_z[t, pl.ds(pl.multiple_of(z * 16, 16), 16), :].astype(F32)
        for d in range(1, NZ):
            reduce_z(t, d).wait_recv()
        for d in range(1, NZ):
            total += recv_z[t, d - 1].astype(F32)
        out[t] = total

    def one_block(b, carry):
        t, k = b // 2, lax.rem(b, 2)
        half = lax.rem(core + k, 2)

        @pl.when(k == 0)
        def _():
            for d in range(1, NX):
                gather_x(t, d).wait_recv()

        @pl.when(b == 1)
        def _():
            for j in range(NY):
                pupil_core(j).wait_recv()

        rows = pl.ds(pl.multiple_of(half * 1024, 1024), 1024)
        grads = source_block(
            32, 4, e[half], spec[t], pupil[rows, :], right[...], left[...], left_t[...], right_t[...], cot[t]
        )
        added = [dot(et[half], g) for g in grads]

        @pl.when(k == 0)
        def _():
            for i in range(NX):
                acc[i * 128 : i * 128 + 128, :] = added[i]

        @pl.when(k == 1)
        def _():
            for i in range(NX):
                send_x[t, i * 128 : i * 128 + 128, :] = (acc[i * 128 : i * 128 + 128, :] + added[i]).astype(BF)
            for d in (2, 1, 3):
                reduce_x(t, d).start()

        @pl.when(b == 4)
        def _():
            turn_x(0)

        @pl.when(b == 6)
        def _():
            turn_x(1)

        return carry

    lax.fori_loop(0, 8, one_block, 0)
    turn_x(2)
    turn_z(0)
    turn_z(1)
    turn_x(3)
    turn_z(2)
    turn_z(3)

    for t in range(4):
        for d in range(1, NZ):
            gather_z(t, d).wait_send()
            reduce_z(t, d).wait_send()
        for d in range(1, NX):
            gather_x(t, d).wait_send()
            reduce_x(t, d).wait_send()
    for d in range(1, NY):
        pupil_y(d).wait_send()
    for j in range(NY):
        pupil_core(j).wait_send()


def shards(spectra, cotangent, pupil_field, source_grid, cutoff, stencil, interp_weights, source_weight):
    own_spec = spectra.reshape(4, 8, 2, 2, 128).transpose(0, 1, 3, 2, 4).reshape(64, 2, 128)
    own_pupil = pupil_field.reshape(8, 2, 32, 128).transpose(0, 2, 1, 3).reshape(256, 2, 128)
    vmem = pl.BlockSpec(memory_space=pltpu.VMEM)
    hbm = pl.BlockSpec(memory_space=pl.ANY)
    dma = pltpu.SemaphoreType.DMA
    result = pl.pallas_call(
        kernel,
        out_shape=jax.ShapeDtypeStruct((4, 16, 256), F32),
        in_specs=[hbm] * 12,
        out_specs=vmem,
        scratch_shapes=[
            pltpu.VMEM((64, 2, 128), BF),
            pltpu.VMEM((256, 2, 128), BF),
            pltpu.VMEM((4, 128, 128), F32),
            pltpu.VMEM((4, 64), jnp.int32),
            pltpu.VMEM((4, 64), BF),
            pltpu.VMEM((1, 64), F32),
            pltpu.SMEM((2, 64), jnp.int32),
            pltpu.SMEM((64,), jnp.int32),
            pltpu.VMEM((256, 512), BF),
            pltpu.VMEM((256, 128), BF),
            pltpu.VMEM((128, 256), BF),
            pltpu.VMEM((512, 256), BF),
            pltpu.VMEM((4, 16, 256), BF),
            pltpu.VMEM((4, 512, 256), BF),
            pltpu.VMEM((2048, 256), BF),
            pltpu.VMEM((2, 256, 128), BF),
            pltpu.VMEM((2, 128, 256), BF),
            pltpu.VMEM((512, 256), F32),
            pltpu.VMEM((4, 512, 256), BF),
            pltpu.VMEM((4, 3, 128, 256), BF),
            pltpu.VMEM((4, 128, 256), BF),
            pltpu.VMEM((4, 7, 16, 256), BF),
            dma((12,)), pltpu.SemaphoreType.REGULAR,
            dma((4, 7)), dma((4, 7)), dma((4, 3)), dma((4, 3)),
            dma((3,)), dma((3,)), dma((4,)), dma((4,)),
            dma((4, 3)), dma((4, 3)), dma((4, 7)), dma((4, 7)),
        ],
        compiler_params=pltpu.CompilerParams(
            collective_id=0, has_side_effects=True, vmem_limit_bytes=56 << 20
        ),
    )(
        own_spec, own_pupil, cotangent, stencil.T, interp_weights.T, source_weight.reshape(1, 64), source_grid.T, cutoff,
        *[jnp.asarray(v) for v in dft_matrices()],
    )
    return result.reshape(4, 8, 2, 2, 128).transpose(0, 1, 3, 2, 4).reshape(4, 8, 2, 256)


def solution(mesh):
    placed = (
        P("tile", "angle", None, "src"),
        P("tile", None, None),
        P(("angle", "src", "tile"), None, None),
        P(("angle", "src"), None),
        P(("angle", "src")),
        P(("angle", "src"), None),
        P(("angle", "src"), None),
        P(("angle", "src")),
    )
    return jax.shard_map(
        shards, mesh=mesh, in_specs=placed, out_specs=P("tile", "angle", None, "src"), check_vma=False
    )
```

```python
import functools
import math

import jax
import jax.numpy as jnp
import ml_dtypes
import numpy as np
from jax import lax
from jax.experimental import pallas as pl
from jax.experimental.pallas import tpu as pltpu
from jax.sharding import PartitionSpec as P

FQ = 64
NP = 128
NX, NY, NZ = 4, 4, 8
BF = jnp.bfloat16
F32 = jnp.float32
MESH = pl.DeviceIdType.MESH
FAR_FIRST = (4, 3, 5, 2, 6, 1, 7)
GROUPS = {32: 4, 64: 8}


def dft_matrices():
    f = np.arange(FQ) - FQ // 2
    phase = np.mod(np.arange(NP)[:, None] * f[None, :], NP) * (2 * math.pi / NP)
    c, s = np.cos(phase) / math.sqrt(FQ), np.sin(phase) / math.sqrt(FQ)
    right = np.zeros((2, 2, 64, 2, 2, 128))
    left = np.zeros((2, 128, 2, 2, 32))
    for p in range(2):
        right[0, p, :, p, 0], right[0, p, :, p, 1] = c.T, s.T
        right[1, p, :, p, 0], right[1, p, :, p, 1] = -s.T, c.T
        left[0, :, p, 0], left[0, :, p, 1] = c[:, p::2], -s[:, p::2]
        left[1, :, p, 0], left[1, :, p, 1] = s[:, p::2], c[:, p::2]
    right, left = right.reshape(256, 512), left.reshape(256, 128)
    return [np.ascontiguousarray(v).astype(ml_dtypes.bfloat16) for v in (right, left, left.T, right.T)]


def dot(a, b):
    return jnp.dot(a, b, preferred_element_type=F32)


def join(values, axis):
    return jnp.concatenate(values, axis=axis)


def source_block(n, h, e, spec, pupil, right, left, left_t, right_t, cot):
    m = n // h
    mixed = [dot(e, spec[x * 128 : x * 128 + 128]) for x in range(NX)]
    pupils, halves = [], []
    for g in range(h):
        p = pupil[g * m * 32 : (g + 1) * m * 32]
        pr, pi = p[:, :128].astype(F32), p[:, 128:].astype(F32)
        pupils.append((pr, pi))
        own = join([mixed[x][s * 8 : s * 8 + 8] for s in range(g * m, (g + 1) * m) for x in range(NX)], 0)
        mr, mi = own[:, :128], own[:, 128:]
        halves.append(join([(pr * mr - pi * mi).astype(BF), (pr * mi + pi * mr).astype(BF)], 1))
    halves = [dot(field, right).astype(BF) for field in halves]
    wide = join([cot, cot], 1)
    wide = join([wide, wide], 0)
    adjoints = []
    for q in range(n // 2):
        pair = []
        for s in (2 * q, 2 * q + 1):
            half, row = halves[s // m], s % m * 32
            pair.append(join([half[row : row + 32, c * 128 : c * 128 + 128] for c in range(4)], 0))
        adjoints.append((dot(left, join(pair, 1)) * wide).astype(BF))
    backs = [dot(left_t, adjoint).astype(BF) for adjoint in adjoints]
    rows = []
    for back in backs:
        for s in range(2):
            rows.append(join([back[c * 32 : c * 32 + 32, s * 128 : s * 128 + 128] for c in range(4)], 1))
    spectra = [dot(join(rows[g * m : (g + 1) * m], 0), right_t) for g in range(h)]
    grads = []
    for (pr, pi), spectrum in zip(pupils, spectra):
        br, bi = spectrum[:, :128], spectrum[:, 128:]
        grads.append(join([pr * br + pi * bi, pr * bi - pi * br], 1))
    return [
        join([grads[s // m][s % m * 32 + x * 8 : s % m * 32 + x * 8 + 8] for s in range(n)], 0).astype(BF)
        for x in range(NX)
    ]


def kernel(
    spec_hbm, pupil_hbm, cot_hbm, stencil_hbm, interp_hbm, weight_hbm, grid_hbm, cutoff_hbm,
    right_hbm, left_hbm, left_t_hbm, right_t_hbm,
    out,
    raw_spec, raw_pupil, cot, stencil, interp, weight, grid, cutoff, right, left, left_t, right_t,
    own_spec, spec, pupil, e, et, acc, send_x, recv_x, send_z, recv_z,
    in_sem, hello, zs_sem, zr_sem, xs_sem, xr_sem, ps_sem, pr_sem, cs_sem, cr_sem, rxs_sem, rxr_sem, rzs_sem, rzr_sem,
):
    angle, src, tile = lax.axis_index("angle"), lax.axis_index("src"), lax.axis_index("tile")
    x, z = src // 4, angle * 4 + lax.rem(src, 4)
    y, core = tile // 2, lax.rem(tile, 2)

    def at_x(d):
        return {"src": lax.rem(x + d, NX) * 4 + lax.rem(src, 4)}

    def at_z(d):
        w = lax.rem(z + d, NZ)
        return {"angle": w // 4, "src": x * 4 + lax.rem(w, 4)}

    def at_y(d):
        return {"tile": lax.rem(y + d, NY) * 2 + core}

    twin = {"tile": y * 2 + 1 - core}
    peers = [at_z(d) for d in FAR_FIRST] + [at_x(d) for d in (2, 1, 3)] + [at_y(d) for d in (2, 1, 3)]
    barrier = pltpu.get_barrier_semaphore()
    for peer in peers:
        pl.semaphore_signal(barrier, inc=1, device_id=peer, device_id_type=MESH)

    @pl.when(core == 0)
    def _():
        pl.semaphore_signal(barrier, inc=1, device_id=twin, device_id_type=MESH)

    pairs = [
        (spec_hbm, raw_spec), (grid_hbm, grid), (cutoff_hbm, cutoff), (pupil_hbm, raw_pupil), (stencil_hbm, stencil),
        (interp_hbm, interp), (weight_hbm, weight), (right_hbm, right), (left_hbm, left), (cot_hbm, cot),
        (left_t_hbm, left_t), (right_t_hbm, right_t),
    ]
    loads = [pltpu.make_async_copy(a, b, in_sem.at[i]) for i, (a, b) in enumerate(pairs)]
    for load in loads:
        load.start()

    loads[0].wait()
    for t in range(4):
        part = raw_spec[t * 16 : t * 16 + 16]
        own_spec[t] = join([part[:, 0], part[:, 1]], 1)

    pl.semaphore_wait(barrier, len(peers) + core)

    @pl.when(core == 1)
    def _():
        pl.semaphore_signal(hello, inc=1, device_id=twin, device_id_type=MESH)

    def remote(src_ref, dst_ref, send, recv, peer):
        return pltpu.make_async_remote_copy(
            src_ref=src_ref, dst_ref=dst_ref, send_sem=send, recv_sem=recv, device_id=peer, device_id_type=MESH
        )

    zrows = pl.ds(pl.multiple_of(z * 16, 16), 16)
    xrows = pl.ds(pl.multiple_of(x * 128, 128), 128)

    def gather_z(t, d):
        return remote(own_spec.at[t], spec.at[t, x, zrows, :], zs_sem.at[t, d - 1], zr_sem.at[t, d - 1], at_z(d))

    def gather_x(t, d):
        rows = spec.at[t, x]
        return remote(rows, rows, xs_sem.at[t, d - 1], xr_sem.at[t, d - 1], at_x(d))

    def first_x(t, d):
        return remote(own_spec.at[t], spec.at[t, x, zrows, :], xs_sem.at[t, d - 1], xr_sem.at[t, d - 1], at_x(d))

    def then_z(t, d):
        rows = spec.at[t, :, zrows, :]
        return remote(rows, rows, zs_sem.at[t, d - 1], zr_sem.at[t, d - 1], at_z(d))

    def forward(t):
        for d in range(1, NX):
            first_x(t, d).wait_recv()
        for d in FAR_FIRST:
            then_z(t, d).start()

    def pupil_rows(yy):
        return pl.ds(pl.multiple_of((core * 4 + yy) * 256, 256), 256)

    def pupil_y(d):
        rows = pupil.at[pupil_rows(y), :]
        return remote(rows, rows, ps_sem.at[d - 1], pr_sem.at[d - 1], at_y(d))

    def pupil_core(j):
        rows = pupil.at[pupil_rows(lax.rem(y + j, NY)), :]
        return remote(rows, rows, cs_sem.at[j], cr_sem.at[j], twin)

    for d in FAR_FIRST:
        gather_z(0, d).start()
    for d in (2, 1, 3):
        first_x(2, d).start()
    for d in (2, 1, 3):
        first_x(3, d).start()

    for load in loads[1:4]:
        load.wait()
    lane = lax.broadcasted_iota(jnp.int32, (32, 128), 1)
    fa = 2 * lax.broadcasted_iota(jnp.int32, (32, 128), 0) + (lane >> 6) - 32
    fb = (lane & 63) - 32

    def mask(s8, carry):
        s = tile * 8 + s8
        da, db = fa + grid[0, s], fb + grid[1, s]
        inside = da * da + db * db <= cutoff[s]
        inside = join([inside, inside], 1)
        part = raw_pupil[pl.ds(pl.multiple_of(s8 * 32, 32), 32)]
        value = join([part[:, 0], part[:, 1]], 1).astype(F32)
        rows = pl.ds(pl.multiple_of((core * 4 + y) * 256 + s8 * 32, 32), 32)
        pupil[rows, :] = jnp.where(inside, value, 0.0).astype(BF)
        return carry

    lax.fori_loop(0, 8, mask, 0)

    for d in (2, 1, 3):
        pupil_y(d).start()
    for d in FAR_FIRST:
        gather_z(1, d).start()
    for t in range(4):
        spec[t, x, zrows, :] = own_spec[t]

    for load in loads[4:7]:
        load.wait()
    c = lax.broadcasted_iota(jnp.int32, (128, 64), 0)
    k_of = (c >> 6) * 8 + ((c >> 1) & 7)
    mix = jnp.zeros((128, 64), F32)
    for j in range(4):
        mix += jnp.where(stencil[j : j + 1, :] == k_of, interp[j : j + 1, :].astype(F32), 0.0)
    scaled = (mix * (weight[...] * (2.0 / math.sqrt(2048)))).astype(BF)
    mix = mix.astype(BF)
    c = lax.broadcasted_iota(jnp.int32, (128, 256), 0)
    col = lax.broadcasted_iota(jnp.int32, (128, 256), 1)
    hit = (col & 7) == ((c >> 4) & 3) * 2 + (c & 1)
    source_at = lax.broadcasted_iota(jnp.int32, (64, 256), 0)
    col = lax.broadcasted_iota(jnp.int32, (64, 256), 1)
    source_of = (col >> 6) * 16 + ((col >> 3) & 7)
    for k in range(2):
        pick = (source_of + k * 8 == source_at).astype(BF)
        et[:, k * 256 : k * 256 + 256] = jnp.where(hit, dot(scaled, pick), 0.0).astype(BF)
        e[k * 256 : k * 256 + 256, :] = jnp.where(hit, dot(mix, pick), 0.0).T.astype(BF)

    for load in loads[7:]:
        load.wait()

    for d in range(1, NZ):
        gather_z(0, d).wait_recv()
    for d in (2, 1, 3):
        gather_x(0, d).start()

    for d in range(1, NZ):
        gather_z(1, d).wait_recv()
    for d in (2, 1, 3):
        gather_x(1, d).start()

    forward(2)

    @pl.when(core == 0)
    def _():
        pl.semaphore_wait(hello, 1)

    pupil_core(0).start()
    for d in range(1, NY):
        pupil_y(d).wait_recv()
        pupil_core(NY - d).start()

    def reduce_x(t, d):
        to = lax.rem(x + d, NX)
        rows = send_x.at[t, pl.ds(pl.multiple_of(to * 128, 128), 128), :]
        return remote(rows, recv_x.at[t, d - 1], rxs_sem.at[t, d - 1], rxr_sem.at[t, d - 1], at_x(d))

    def z_block(d):
        return lax.rem(z + d, NZ) * 16

    def reduce_z(t, d):
        rows = send_z.at[t, pl.ds(pl.multiple_of(z_block(d), 16), 16), :]
        return remote(rows, recv_z.at[t, d - 1], rzs_sem.at[t, d - 1], rzr_sem.at[t, d - 1], at_z(d))

    def turn_x(t):
        for d in range(1, NX):
            reduce_x(t, d).wait_recv()
        for d in FAR_FIRST + (0,):
            rows = pl.ds(pl.multiple_of(z_block(d), 16), 16)
            total = send_x[t, pl.ds(pl.multiple_of(x * 128 + z_block(d), 16), 16), :].astype(F32)
            for w in range(NX - 1):
                total += recv_x[t, w, rows, :].astype(F32)
            send_z[t, rows, :] = total.astype(BF)
            if d:
                reduce_z(t, d).start()

    def turn_z(t):
        total = send_z[t, pl.ds(pl.multiple_of(z * 16, 16), 16), :].astype(F32)
        for d in range(1, NZ):
            reduce_z(t, d).wait_recv()
        for d in range(1, NZ):
            total += recv_z[t, d - 1].astype(F32)
        out[t] = total

    def sums(n, first, t):
        grads = source_block(
            n, GROUPS[n], e[pl.ds(pl.multiple_of(first * 8, 256), n * 8), :], spec[t].reshape(512, 256),
            pupil[pl.ds(pl.multiple_of(first * 32, 1024), n * 32), :],
            right[...], left[...], left_t[...], right_t[...], cot[t],
        )
        weights = et[:, pl.ds(pl.multiple_of(first * 8, 256), n * 8)]
        return [dot(weights, g) for g in grads]

    for d in range(1, NX):
        gather_x(0, d).wait_recv()

    def first_tile(k, carry):
        @pl.when(k == 1)
        def _():
            forward(3)
            for j in range(NY):
                pupil_core(j).wait_recv()

        added = sums(32, lax.rem(core + k, 2) * 32, 0)
        for i in range(NX):
            rows = pl.ds(i * 128, 128)
            acc[rows, :] = acc[rows, :] * k.astype(F32) + added[i]
        return carry

    acc[...] = jnp.zeros_like(acc)
    lax.fori_loop(0, 2, first_tile, 0)
    send_x[0] = acc[...].astype(BF)
    for d in (2, 1, 3):
        reduce_x(0, d).start()

    def one_tile(t, carry):
        @pl.when(t == 1)
        def _():
            for d in range(1, NX):
                gather_x(t, d).wait_recv()

        @pl.when(t > 1)
        def _():
            for d in range(1, NZ):
                then_z(t, d).wait_recv()

        added = sums(64, 0, t)
        for i in range(NX):
            send_x[t, i * 128 : i * 128 + 128, :] = added[i].astype(BF)
        for d in (2, 1, 3):
            reduce_x(t, d).start()

        @pl.when(t == 2)
        def _():
            turn_x(0)

        return carry

    lax.fori_loop(1, 4, one_tile, 0)
    turn_x(1)
    turn_x(2)
    turn_z(0)
    turn_z(1)
    turn_x(3)
    turn_z(2)
    turn_z(3)

    for t in range(4):
        for d in range(1, NZ):
            (then_z if t in (2, 3) else gather_z)(t, d).wait_send()
            reduce_z(t, d).wait_send()
        for d in range(1, NX):
            (first_x if t in (2, 3) else gather_x)(t, d).wait_send()
            reduce_x(t, d).wait_send()
    for d in range(1, NY):
        pupil_y(d).wait_send()
    for j in range(NY):
        pupil_core(j).wait_send()


def shards(spectra, cotangent, pupil_field, source_grid, cutoff, stencil, interp_weights, source_weight):
    own_spec = spectra.reshape(4, 8, 2, 2, 128).transpose(0, 1, 3, 2, 4).reshape(64, 2, 128)
    own_pupil = pupil_field.reshape(8, 2, 32, 128).transpose(0, 2, 1, 3).reshape(256, 2, 128)
    vmem = pl.BlockSpec(memory_space=pltpu.VMEM)
    hbm = pl.BlockSpec(memory_space=pl.ANY)
    dma = pltpu.SemaphoreType.DMA
    result = pl.pallas_call(
        kernel,
        out_shape=jax.ShapeDtypeStruct((4, 16, 256), F32),
        in_specs=[hbm] * 12,
        out_specs=vmem,
        scratch_shapes=[
            pltpu.VMEM((64, 2, 128), BF),
            pltpu.VMEM((256, 2, 128), BF),
            pltpu.VMEM((4, 128, 128), F32),
            pltpu.VMEM((4, 64), jnp.int32),
            pltpu.VMEM((4, 64), BF),
            pltpu.VMEM((1, 64), F32),
            pltpu.SMEM((2, 64), jnp.int32),
            pltpu.SMEM((64,), jnp.int32),
            pltpu.VMEM((256, 512), BF),
            pltpu.VMEM((256, 128), BF),
            pltpu.VMEM((128, 256), BF),
            pltpu.VMEM((512, 256), BF),
            pltpu.VMEM((4, 16, 256), BF),
            pltpu.VMEM((4, NX, 128, 256), BF),
            pltpu.VMEM((2048, 256), BF),
            pltpu.VMEM((512, 128), BF),
            pltpu.VMEM((128, 512), BF),
            pltpu.VMEM((512, 256), F32),
            pltpu.VMEM((4, 512, 256), BF),
            pltpu.VMEM((4, 3, 128, 256), BF),
            pltpu.VMEM((4, 128, 256), BF),
            pltpu.VMEM((4, 7, 16, 256), BF),
            dma((12,)), pltpu.SemaphoreType.REGULAR,
            dma((4, 7)), dma((4, 7)), dma((4, 3)), dma((4, 3)),
            dma((3,)), dma((3,)), dma((4,)), dma((4,)),
            dma((4, 3)), dma((4, 3)), dma((4, 7)), dma((4, 7)),
        ],
        compiler_params=pltpu.CompilerParams(
            collective_id=0, has_side_effects=True, vmem_limit_bytes=56 << 20
        ),
    )(
        own_spec, own_pupil, cotangent, stencil.T, interp_weights.T, source_weight.reshape(1, 64), source_grid.T, cutoff,
        *[jnp.asarray(v) for v in dft_matrices()],
    )
    return result.reshape(4, 8, 2, 2, 128).transpose(0, 1, 3, 2, 4).reshape(4, 8, 2, 256)


def solution(mesh):
    placed = (
        P("tile", "angle", None, "src"),
        P("tile", None, None),
        P(("angle", "src", "tile"), None, None),
        P(("angle", "src"), None),
        P(("angle", "src")),
        P(("angle", "src"), None),
        P(("angle", "src"), None),
        P(("angle", "src")),
    )
    return jax.shard_map(
        shards, mesh=mesh, in_specs=placed, out_specs=P("tile", "angle", None, "src"), check_vma=False
    )
```

```python
import functools
import math

import jax
import jax.numpy as jnp
import ml_dtypes
import numpy as np
from jax import lax
from jax.experimental import pallas as pl
from jax.experimental.pallas import tpu as pltpu
from jax.sharding import PartitionSpec as P

FQ = 64
NP = 128
NX, NY, NZ = 4, 4, 8
BF = jnp.bfloat16
F32 = jnp.float32
MESH = pl.DeviceIdType.MESH
FAR_FIRST = (4, 3, 5, 2, 6, 1, 7)
GROUPS = {32: 4, 64: 8}


def dft_matrices():
    f = np.arange(FQ) - FQ // 2
    phase = np.mod(np.arange(NP)[:, None] * f[None, :], NP) * (2 * math.pi / NP)
    c, s = np.cos(phase) / math.sqrt(FQ), np.sin(phase) / math.sqrt(FQ)
    right = np.zeros((2, 2, 64, 2, 2, 128))
    left = np.zeros((2, 128, 2, 2, 32))
    for p in range(2):
        right[0, p, :, p, 0], right[0, p, :, p, 1] = c.T, s.T
        right[1, p, :, p, 0], right[1, p, :, p, 1] = -s.T, c.T
        left[0, :, p, 0], left[0, :, p, 1] = c[:, p::2], -s[:, p::2]
        left[1, :, p, 0], left[1, :, p, 1] = s[:, p::2], c[:, p::2]
    right, left = right.reshape(256, 512), left.reshape(256, 128)
    return [np.ascontiguousarray(v).astype(ml_dtypes.bfloat16) for v in (right, left, left.T, right.T)]


def dot(a, b):
    return jnp.dot(a, b, preferred_element_type=F32)


def join(values, axis):
    return jnp.concatenate(values, axis=axis)


def source_block(n, h, e, spec, pupil, right, left, left_t, right_t, cot):
    m = n // h
    mixed = [dot(e, spec[x * 128 : x * 128 + 128]) for x in range(NX)]
    pupils, halves = [], []
    for g in range(h):
        p = pupil[g * m * 32 : (g + 1) * m * 32]
        pr, pi = p[:, :128].astype(F32), p[:, 128:].astype(F32)
        pupils.append((pr, pi))
        own = join([mixed[x][s * 8 : s * 8 + 8] for s in range(g * m, (g + 1) * m) for x in range(NX)], 0)
        mr, mi = own[:, :128], own[:, 128:]
        halves.append(join([(pr * mr - pi * mi).astype(BF), (pr * mi + pi * mr).astype(BF)], 1))
    halves = [dot(field, right).astype(BF) for field in halves]
    wide = join([cot, cot], 1)
    wide = join([wide, wide], 0)
    adjoints = []
    for q in range(n // 2):
        pair = []
        for s in (2 * q, 2 * q + 1):
            half, row = halves[s // m], s % m * 32
            pair.append(join([half[row : row + 32, c * 128 : c * 128 + 128] for c in range(4)], 0))
        adjoints.append((dot(left, join(pair, 1)) * wide).astype(BF))
    backs = [dot(left_t, adjoint).astype(BF) for adjoint in adjoints]
    rows = []
    for back in backs:
        for s in range(2):
            rows.append(join([back[c * 32 : c * 32 + 32, s * 128 : s * 128 + 128] for c in range(4)], 1))
    spectra = [dot(join(rows[g * m : (g + 1) * m], 0), right_t) for g in range(h)]
    grads = []
    for (pr, pi), spectrum in zip(pupils, spectra):
        br, bi = spectrum[:, :128], spectrum[:, 128:]
        grads.append(join([pr * br + pi * bi, pr * bi - pi * br], 1))
    return [
        join([grads[s // m][s % m * 32 + x * 8 : s % m * 32 + x * 8 + 8] for s in range(n)], 0).astype(BF)
        for x in range(NX)
    ]


def kernel(
    spec_hbm, pupil_hbm, cot_hbm, stencil_hbm, interp_hbm, weight_hbm, grid_hbm, cutoff_hbm,
    right_hbm, left_hbm, left_t_hbm, right_t_hbm,
    out,
    raw_spec, raw_pupil, cot, stencil, interp, weight, grid, cutoff, right, left, left_t, right_t,
    own_spec, spec, pupil, e, et, acc, send_x, recv_x, send_z, recv_z,
    in_sem, hello, zs_sem, zr_sem, xs_sem, xr_sem, ps_sem, pr_sem, cs_sem, cr_sem, rxs_sem, rxr_sem, rzs_sem, rzr_sem,
):
    angle, src, tile = lax.axis_index("angle"), lax.axis_index("src"), lax.axis_index("tile")
    x, z = src // 4, angle * 4 + lax.rem(src, 4)
    y, core = tile // 2, lax.rem(tile, 2)

    def at_x(d):
        return {"src": lax.rem(x + d, NX) * 4 + lax.rem(src, 4)}

    def at_z(d):
        w = lax.rem(z + d, NZ)
        return {"angle": w // 4, "src": x * 4 + lax.rem(w, 4)}

    def at_y(d):
        return {"tile": lax.rem(y + d, NY) * 2 + core}

    twin = {"tile": y * 2 + 1 - core}
    peers = [at_z(d) for d in FAR_FIRST] + [at_x(d) for d in (2, 1, 3)] + [at_y(d) for d in (2, 1, 3)]
    barrier = pltpu.get_barrier_semaphore()
    for peer in peers:
        pl.semaphore_signal(barrier, inc=1, device_id=peer, device_id_type=MESH)

    @pl.when(core == 0)
    def _():
        pl.semaphore_signal(barrier, inc=1, device_id=twin, device_id_type=MESH)

    pairs = [
        (spec_hbm, raw_spec), (grid_hbm, grid), (cutoff_hbm, cutoff), (pupil_hbm, raw_pupil), (stencil_hbm, stencil),
        (interp_hbm, interp), (weight_hbm, weight), (right_hbm, right), (left_hbm, left), (cot_hbm, cot),
        (left_t_hbm, left_t), (right_t_hbm, right_t),
    ]
    loads = [pltpu.make_async_copy(a, b, in_sem.at[i]) for i, (a, b) in enumerate(pairs)]
    for load in loads:
        load.start()

    loads[0].wait()
    for t in range(4):
        part = raw_spec[t * 16 : t * 16 + 16]
        own_spec[t] = join([part[:, 0], part[:, 1]], 1)

    for load in loads[1:4]:
        load.wait()
    lane = lax.broadcasted_iota(jnp.int32, (32, 128), 1)
    fa = 2 * lax.broadcasted_iota(jnp.int32, (32, 128), 0) + (lane >> 6) - 32
    fb = (lane & 63) - 32

    def mask(s8, carry):
        s = tile * 8 + s8
        da, db = fa + grid[0, s], fb + grid[1, s]
        inside = da * da + db * db <= cutoff[s]
        inside = join([inside, inside], 1)
        part = raw_pupil[pl.ds(pl.multiple_of(s8 * 32, 32), 32)]
        value = join([part[:, 0], part[:, 1]], 1).astype(F32)
        rows = pl.ds(pl.multiple_of((core * 4 + y) * 256 + s8 * 32, 32), 32)
        pupil[rows, :] = jnp.where(inside, value, 0.0).astype(BF)
        return carry

    lax.fori_loop(0, 8, mask, 0)

    pl.semaphore_wait(barrier, len(peers) + core)

    @pl.when(core == 1)
    def _():
        pl.semaphore_signal(hello, inc=1, device_id=twin, device_id_type=MESH)

    def remote(src_ref, dst_ref, send, recv, peer):
        return pltpu.make_async_remote_copy(
            src_ref=src_ref, dst_ref=dst_ref, send_sem=send, recv_sem=recv, device_id=peer, device_id_type=MESH
        )

    zrows = pl.ds(pl.multiple_of(z * 16, 16), 16)
    xrows = pl.ds(pl.multiple_of(x * 128, 128), 128)

    def gather_z(t, d):
        return remote(own_spec.at[t], spec.at[t, x, zrows, :], zs_sem.at[t, d - 1], zr_sem.at[t, d - 1], at_z(d))

    def gather_x(t, d):
        rows = spec.at[t, x]
        return remote(rows, rows, xs_sem.at[t, d - 1], xr_sem.at[t, d - 1], at_x(d))

    def first_x(t, d):
        return remote(own_spec.at[t], spec.at[t, x, zrows, :], xs_sem.at[t, d - 1], xr_sem.at[t, d - 1], at_x(d))

    def then_z(t, d):
        rows = spec.at[t, :, zrows, :]
        return remote(rows, rows, zs_sem.at[t, d - 1], zr_sem.at[t, d - 1], at_z(d))

    def forward(t):
        for d in range(1, NX):
            first_x(t, d).wait_recv()
        for d in FAR_FIRST:
            then_z(t, d).start()

    def pupil_rows(yy):
        return pl.ds(pl.multiple_of((core * 4 + yy) * 256, 256), 256)

    def pupil_y(d):
        rows = pupil.at[pupil_rows(y), :]
        return remote(rows, rows, ps_sem.at[d - 1], pr_sem.at[d - 1], at_y(d))

    def pupil_core(j):
        rows = pupil.at[pupil_rows(lax.rem(y + j, NY)), :]
        return remote(rows, rows, cs_sem.at[j], cr_sem.at[j], twin)

    for d in FAR_FIRST:
        gather_z(0, d).start()
    for d in (2, 1, 3):
        first_x(2, d).start()
    for d in (2, 1, 3):
        first_x(3, d).start()

    for d in (2, 1, 3):
        pupil_y(d).start()
    for d in FAR_FIRST:
        gather_z(1, d).start()
    for t in range(4):
        spec[t, x, zrows, :] = own_spec[t]

    for load in loads[4:7]:
        load.wait()
    c = lax.broadcasted_iota(jnp.int32, (128, 64), 0)
    k_of = (c >> 6) * 8 + ((c >> 1) & 7)
    mix = jnp.zeros((128, 64), F32)
    for j in range(4):
        mix += jnp.where(stencil[j : j + 1, :] == k_of, interp[j : j + 1, :].astype(F32), 0.0)
    scaled = (mix * (weight[...] * (2.0 / math.sqrt(2048)))).astype(BF)
    mix = mix.astype(BF)
    c = lax.broadcasted_iota(jnp.int32, (128, 256), 0)
    col = lax.broadcasted_iota(jnp.int32, (128, 256), 1)
    hit = (col & 7) == ((c >> 4) & 3) * 2 + (c & 1)
    source_at = lax.broadcasted_iota(jnp.int32, (64, 256), 0)
    col = lax.broadcasted_iota(jnp.int32, (64, 256), 1)
    source_of = (col >> 6) * 16 + ((col >> 3) & 7)
    for k in range(2):
        pick = (source_of + k * 8 == source_at).astype(BF)
        et[:, k * 256 : k * 256 + 256] = jnp.where(hit, dot(scaled, pick), 0.0).astype(BF)
        e[k * 256 : k * 256 + 256, :] = jnp.where(hit, dot(mix, pick), 0.0).T.astype(BF)

    for load in loads[7:]:
        load.wait()

    for d in range(1, NZ):
        gather_z(0, d).wait_recv()
    for d in (2, 1, 3):
        gather_x(0, d).start()

    for d in range(1, NZ):
        gather_z(1, d).wait_recv()
    for d in (2, 1, 3):
        gather_x(1, d).start()

    forward(2)

    @pl.when(core == 0)
    def _():
        pl.semaphore_wait(hello, 1)

    pupil_core(0).start()
    for d in range(1, NY):
        pupil_y(d).wait_recv()
        pupil_core(NY - d).start()

    def reduce_x(t, d):
        to = lax.rem(x + d, NX)
        rows = send_x.at[t, pl.ds(pl.multiple_of(to * 128, 128), 128), :]
        return remote(rows, recv_x.at[t, d - 1], rxs_sem.at[t, d - 1], rxr_sem.at[t, d - 1], at_x(d))

    def z_block(d):
        return lax.rem(z + d, NZ) * 16

    def reduce_z(t, d):
        rows = send_z.at[t, pl.ds(pl.multiple_of(z_block(d), 16), 16), :]
        return remote(rows, recv_z.at[t, d - 1], rzs_sem.at[t, d - 1], rzr_sem.at[t, d - 1], at_z(d))

    def turn_x(t):
        for d in range(1, NX):
            reduce_x(t, d).wait_recv()
        for d in FAR_FIRST + (0,):
            rows = pl.ds(pl.multiple_of(z_block(d), 16), 16)
            total = send_x[t, pl.ds(pl.multiple_of(x * 128 + z_block(d), 16), 16), :].astype(F32)
            for w in range(NX - 1):
                total += recv_x[t, w, rows, :].astype(F32)
            send_z[t, rows, :] = total.astype(BF)
            if d:
                reduce_z(t, d).start()

    def turn_z(t):
        total = send_z[t, pl.ds(pl.multiple_of(z * 16, 16), 16), :].astype(F32)
        for d in range(1, NZ):
            reduce_z(t, d).wait_recv()
        for d in range(1, NZ):
            total += recv_z[t, d - 1].astype(F32)
        out[t] = total

    def sums(n, first, t):
        grads = source_block(
            n, GROUPS[n], e[pl.ds(pl.multiple_of(first * 8, 256), n * 8), :], spec[t].reshape(512, 256),
            pupil[pl.ds(pl.multiple_of(first * 32, 1024), n * 32), :],
            right[...], left[...], left_t[...], right_t[...], cot[t],
        )
        weights = et[:, pl.ds(pl.multiple_of(first * 8, 256), n * 8)]
        return [dot(weights, g) for g in grads]

    for d in range(1, NX):
        gather_x(0, d).wait_recv()

    def first_tile(k, carry):
        @pl.when(k == 1)
        def _():
            forward(3)
            for j in range(NY):
                pupil_core(j).wait_recv()

        added = sums(32, lax.rem(core + k, 2) * 32, 0)
        for i in range(NX):
            rows = pl.ds(i * 128, 128)
            acc[rows, :] = acc[rows, :] * k.astype(F32) + added[i]
        return carry

    acc[...] = jnp.zeros_like(acc)
    lax.fori_loop(0, 2, first_tile, 0)
    send_x[0] = acc[...].astype(BF)
    for d in (2, 1, 3):
        reduce_x(0, d).start()

    def one_tile(t, carry):
        @pl.when(t == 1)
        def _():
            for d in range(1, NX):
                gather_x(t, d).wait_recv()

        @pl.when(t > 1)
        def _():
            for d in range(1, NZ):
                then_z(t, d).wait_recv()

        added = sums(64, 0, t)
        for i in range(NX):
            send_x[t, i * 128 : i * 128 + 128, :] = added[i].astype(BF)
        for d in (2, 1, 3):
            reduce_x(t, d).start()

        @pl.when(t == 2)
        def _():
            turn_x(0)

        return carry

    lax.fori_loop(1, 4, one_tile, 0)
    turn_x(1)
    turn_x(2)
    turn_z(0)
    turn_z(1)
    turn_x(3)
    turn_z(2)
    for t in range(4):
        for d in range(1, NZ):
            (then_z if t in (2, 3) else gather_z)(t, d).wait_send()
            if t < 3:
                reduce_z(t, d).wait_send()
        for d in range(1, NX):
            (first_x if t in (2, 3) else gather_x)(t, d).wait_send()
            reduce_x(t, d).wait_send()
    for d in range(1, NY):
        pupil_y(d).wait_send()
    for j in range(NY):
        pupil_core(j).wait_send()
    turn_z(3)
    for d in range(1, NZ):
        reduce_z(3, d).wait_send()


def shards(spectra, cotangent, pupil_field, source_grid, cutoff, stencil, interp_weights, source_weight):
    own_spec = spectra.reshape(4, 8, 2, 2, 128).transpose(0, 1, 3, 2, 4).reshape(64, 2, 128)
    own_pupil = pupil_field.reshape(8, 2, 32, 128).transpose(0, 2, 1, 3).reshape(256, 2, 128)
    vmem = pl.BlockSpec(memory_space=pltpu.VMEM)
    hbm = pl.BlockSpec(memory_space=pl.ANY)
    dma = pltpu.SemaphoreType.DMA
    result = pl.pallas_call(
        kernel,
        out_shape=pltpu.VMEM((4, 16, 256), F32),
        in_specs=[hbm] * 12,
        out_specs=vmem,
        scratch_shapes=[
            pltpu.VMEM((64, 2, 128), BF),
            pltpu.VMEM((256, 2, 128), BF),
            pltpu.VMEM((4, 128, 128), F32),
            pltpu.VMEM((4, 64), jnp.int32),
            pltpu.VMEM((4, 64), BF),
            pltpu.VMEM((1, 64), F32),
            pltpu.SMEM((2, 64), jnp.int32),
            pltpu.SMEM((64,), jnp.int32),
            pltpu.VMEM((256, 512), BF),
            pltpu.VMEM((256, 128), BF),
            pltpu.VMEM((128, 256), BF),
            pltpu.VMEM((512, 256), BF),
            pltpu.VMEM((4, 16, 256), BF),
            pltpu.VMEM((4, NX, 128, 256), BF),
            pltpu.VMEM((2048, 256), BF),
            pltpu.VMEM((512, 128), BF),
            pltpu.VMEM((128, 512), BF),
            pltpu.VMEM((512, 256), F32),
            pltpu.VMEM((4, 512, 256), BF),
            pltpu.VMEM((4, 3, 128, 256), BF),
            pltpu.VMEM((4, 128, 256), BF),
            pltpu.VMEM((4, 7, 16, 256), BF),
            dma((12,)), pltpu.SemaphoreType.REGULAR,
            dma((4, 7)), dma((4, 7)), dma((4, 3)), dma((4, 3)),
            dma((3,)), dma((3,)), dma((4,)), dma((4,)),
            dma((4, 3)), dma((4, 3)), dma((4, 7)), dma((4, 7)),
        ],
        compiler_params=pltpu.CompilerParams(
            collective_id=0, has_side_effects=True, vmem_limit_bytes=56 << 20
        ),
    )(
        own_spec, own_pupil, cotangent, stencil.T, interp_weights.T, source_weight.reshape(1, 64), source_grid.T, cutoff,
        *[jnp.asarray(v) for v in dft_matrices()],
    )
    return result.reshape(4, 8, 2, 2, 128).transpose(0, 1, 3, 2, 4).reshape(4, 8, 2, 256)


def solution(mesh):
    placed = (
        P("tile", "angle", None, "src"),
        P("tile", None, None),
        P(("angle", "src", "tile"), None, None),
        P(("angle", "src"), None),
        P(("angle", "src")),
        P(("angle", "src"), None),
        P(("angle", "src"), None),
        P(("angle", "src")),
    )
    return jax.shard_map(
        shards, mesh=mesh, in_specs=placed, out_specs=P("tile", "angle", None, "src"), check_vma=False
    )
```

```python
import functools
import math

import jax
import jax.numpy as jnp
import ml_dtypes
import numpy as np
from jax import lax
from jax.experimental import pallas as pl
from jax.experimental.pallas import tpu as pltpu
from jax.sharding import PartitionSpec as P

FQ = 64
NP = 128
NX, NY, NZ = 4, 4, 8
BF = jnp.bfloat16
F32 = jnp.float32
MESH = pl.DeviceIdType.MESH
FAR_FIRST = (4, 3, 5, 2, 6, 1, 7)
GROUPS = {32: 4, 64: 8}


def dft_matrices():
    f = np.arange(FQ) - FQ // 2
    phase = np.mod(np.arange(NP)[:, None] * f[None, :], NP) * (2 * math.pi / NP)
    c, s = np.cos(phase) / math.sqrt(FQ), np.sin(phase) / math.sqrt(FQ)
    right = np.zeros((2, 2, 64, 2, 2, 128))
    left = np.zeros((2, 128, 2, 2, 32))
    for p in range(2):
        right[0, p, :, p, 0], right[0, p, :, p, 1] = c.T, s.T
        right[1, p, :, p, 0], right[1, p, :, p, 1] = -s.T, c.T
        left[0, :, p, 0], left[0, :, p, 1] = c[:, p::2], -s[:, p::2]
        left[1, :, p, 0], left[1, :, p, 1] = s[:, p::2], c[:, p::2]
    right, left = right.reshape(256, 512), left.reshape(256, 128)
    return [np.ascontiguousarray(v).astype(ml_dtypes.bfloat16) for v in (right, left, left.T, right.T)]


def dot(a, b):
    return jnp.dot(a, b, preferred_element_type=F32)


def join(values, axis):
    return jnp.concatenate(values, axis=axis)


def source_block(n, h, e, spec, pupil, right, left, left_t, right_t, cot):
    m = n // h
    mixed = [dot(e, spec[x * 128 : x * 128 + 128]) for x in range(NX)]
    pupils, halves = [], []
    for g in range(h):
        p = pupil[g * m * 32 : (g + 1) * m * 32]
        pr, pi = p[:, :128].astype(F32), p[:, 128:].astype(F32)
        pupils.append((pr, pi))
        own = join([mixed[x][s * 8 : s * 8 + 8] for s in range(g * m, (g + 1) * m) for x in range(NX)], 0)
        mr, mi = own[:, :128], own[:, 128:]
        halves.append(join([(pr * mr - pi * mi).astype(BF), (pr * mi + pi * mr).astype(BF)], 1))
    halves = [dot(field, right).astype(BF) for field in halves]
    wide = join([cot, cot], 1)
    wide = join([wide, wide], 0)
    adjoints = []
    for q in range(n // 2):
        pair = []
        for s in (2 * q, 2 * q + 1):
            half, row = halves[s // m], s % m * 32
            pair.append(join([half[row : row + 32, c * 128 : c * 128 + 128] for c in range(4)], 0))
        adjoints.append((dot(left, join(pair, 1)) * wide).astype(BF))
    backs = [dot(left_t, adjoint).astype(BF) for adjoint in adjoints]
    rows = []
    for back in backs:
        for s in range(2):
            rows.append(join([back[c * 32 : c * 32 + 32, s * 128 : s * 128 + 128] for c in range(4)], 1))
    spectra = [dot(join(rows[g * m : (g + 1) * m], 0), right_t) for g in range(h)]
    grads = []
    for (pr, pi), spectrum in zip(pupils, spectra):
        br, bi = spectrum[:, :128], spectrum[:, 128:]
        grads.append(join([pr * br + pi * bi, pr * bi - pi * br], 1))
    return [
        join([grads[s // m][s % m * 32 + x * 8 : s % m * 32 + x * 8 + 8] for s in range(n)], 0).astype(BF)
        for x in range(NX)
    ]


def kernel(
    spec_hbm, pupil_hbm, cot_hbm, stencil_hbm, interp_hbm, weight_hbm, grid_hbm, cutoff_hbm,
    right_hbm, left_hbm, left_t_hbm, right_t_hbm,
    out,
    raw_spec, raw_pupil, cot, stencil, interp, weight, grid, cutoff, right, left, left_t, right_t,
    own_spec, spec, pupil, e, et, acc, send_x, recv_x, send_z, recv_z,
    in_sem, hello, zs_sem, zr_sem, xs_sem, xr_sem, ps_sem, pr_sem, cs_sem, cr_sem, rxs_sem, rxr_sem, rzs_sem, rzr_sem,
):
    angle, src, tile = lax.axis_index("angle"), lax.axis_index("src"), lax.axis_index("tile")
    x, z = src // 4, angle * 4 + lax.rem(src, 4)
    y, core = tile // 2, lax.rem(tile, 2)

    def at_x(d):
        return {"src": lax.rem(x + d, NX) * 4 + lax.rem(src, 4)}

    def at_z(d):
        w = lax.rem(z + d, NZ)
        return {"angle": w // 4, "src": x * 4 + lax.rem(w, 4)}

    def at_y(d):
        return {"tile": lax.rem(y + d, NY) * 2 + core}

    twin = {"tile": y * 2 + 1 - core}
    peers = [at_z(d) for d in FAR_FIRST] + [at_x(d) for d in (2, 1, 3)] + [at_y(d) for d in (2, 1, 3)]
    barrier = pltpu.get_barrier_semaphore()
    for peer in peers:
        pl.semaphore_signal(barrier, inc=1, device_id=peer, device_id_type=MESH)

    @pl.when(core == 0)
    def _():
        pl.semaphore_signal(barrier, inc=1, device_id=twin, device_id_type=MESH)

    pairs = [
        (spec_hbm, raw_spec), (grid_hbm, grid), (cutoff_hbm, cutoff), (pupil_hbm, raw_pupil), (stencil_hbm, stencil),
        (interp_hbm, interp), (weight_hbm, weight), (right_hbm, right), (left_hbm, left), (cot_hbm, cot),
        (left_t_hbm, left_t), (right_t_hbm, right_t),
    ]
    loads = [pltpu.make_async_copy(a, b, in_sem.at[i]) for i, (a, b) in enumerate(pairs)]
    for load in loads:
        load.start()

    loads[0].wait()
    for t in range(4):
        part = raw_spec[t * 16 : t * 16 + 16]
        own_spec[t] = join([part[:, 0], part[:, 1]], 1)

    for load in loads[1:4]:
        load.wait()
    lane = lax.broadcasted_iota(jnp.int32, (32, 128), 1)
    fa = 2 * lax.broadcasted_iota(jnp.int32, (32, 128), 0) + (lane >> 6) - 32
    fb = (lane & 63) - 32

    def mask(s8, carry):
        s = tile * 8 + s8
        da, db = fa + grid[0, s], fb + grid[1, s]
        inside = da * da + db * db <= cutoff[s]
        inside = join([inside, inside], 1)
        part = raw_pupil[pl.ds(pl.multiple_of(s8 * 32, 32), 32)]
        value = join([part[:, 0], part[:, 1]], 1).astype(F32)
        rows = pl.ds(pl.multiple_of((core * 4 + y) * 256 + s8 * 32, 32), 32)
        pupil[rows, :] = jnp.where(inside, value, 0.0).astype(BF)
        return carry

    lax.fori_loop(0, 8, mask, 0)

    pl.semaphore_wait(barrier, len(peers) + core)

    @pl.when(core == 1)
    def _():
        pl.semaphore_signal(hello, inc=1, device_id=twin, device_id_type=MESH)

    def remote(src_ref, dst_ref, send, recv, peer):
        return pltpu.make_async_remote_copy(
            src_ref=src_ref, dst_ref=dst_ref, send_sem=send, recv_sem=recv, device_id=peer, device_id_type=MESH
        )

    zrows = pl.ds(pl.multiple_of(z * 16, 16), 16)
    xrows = pl.ds(pl.multiple_of(x * 128, 128), 128)

    def gather_z(t, d):
        return remote(own_spec.at[t], spec.at[t, x, zrows, :], zs_sem.at[t, d - 1], zr_sem.at[t, d - 1], at_z(d))

    def gather_x(t, d):
        rows = spec.at[t, x]
        return remote(rows, rows, xs_sem.at[t, d - 1], xr_sem.at[t, d - 1], at_x(d))

    def first_x(t, d):
        return remote(own_spec.at[t], spec.at[t, x, zrows, :], xs_sem.at[t, d - 1], xr_sem.at[t, d - 1], at_x(d))

    def then_z(t, d):
        rows = spec.at[t, :, zrows, :]
        return remote(rows, rows, zs_sem.at[t, d - 1], zr_sem.at[t, d - 1], at_z(d))

    def forward(t):
        for d in range(1, NX):
            first_x(t, d).wait_recv()
        for d in FAR_FIRST:
            then_z(t, d).start()

    def pupil_rows(yy):
        return pl.ds(pl.multiple_of((core * 4 + yy) * 256, 256), 256)

    def pupil_y(d):
        rows = pupil.at[pupil_rows(y), :]
        return remote(rows, rows, ps_sem.at[d - 1], pr_sem.at[d - 1], at_y(d))

    def pupil_core(j):
        rows = pupil.at[pupil_rows(lax.rem(y + j, NY)), :]
        return remote(rows, rows, cs_sem.at[j], cr_sem.at[j], twin)

    for d in FAR_FIRST:
        gather_z(0, d).start()
    for d in (2, 1, 3):
        first_x(2, d).start()
    for d in (2, 1, 3):
        first_x(3, d).start()

    for d in (2, 1, 3):
        pupil_y(d).start()
    for d in FAR_FIRST:
        gather_z(1, d).start()
    for t in range(4):
        spec[t, x, zrows, :] = own_spec[t]

    for load in loads[4:7]:
        load.wait()
    c = lax.broadcasted_iota(jnp.int32, (128, 64), 0)
    k_of = (c >> 6) * 8 + ((c >> 1) & 7)
    mix = jnp.zeros((128, 64), F32)
    for j in range(4):
        mix += jnp.where(stencil[j : j + 1, :] == k_of, interp[j : j + 1, :].astype(F32), 0.0)
    scaled = (mix * (weight[...] * (2.0 / math.sqrt(2048)))).astype(BF)
    mix = mix.astype(BF)
    c = lax.broadcasted_iota(jnp.int32, (128, 256), 0)
    col = lax.broadcasted_iota(jnp.int32, (128, 256), 1)
    hit = (col & 7) == ((c >> 4) & 3) * 2 + (c & 1)
    source_at = lax.broadcasted_iota(jnp.int32, (64, 256), 0)
    col = lax.broadcasted_iota(jnp.int32, (64, 256), 1)
    source_of = (col >> 6) * 16 + ((col >> 3) & 7)
    for k in range(2):
        pick = (source_of + k * 8 == source_at).astype(BF)
        et[:, k * 256 : k * 256 + 256] = jnp.where(hit, dot(scaled, pick), 0.0).astype(BF)
        e[k * 256 : k * 256 + 256, :] = jnp.where(hit, dot(mix, pick), 0.0).T.astype(BF)

    for load in loads[7:]:
        load.wait()

    for d in range(1, NZ):
        gather_z(0, d).wait_recv()
    for d in (2, 1, 3):
        gather_x(0, d).start()

    for d in range(1, NZ):
        gather_z(1, d).wait_recv()
    for d in (2, 1, 3):
        gather_x(1, d).start()

    forward(2)

    @pl.when(core == 0)
    def _():
        pl.semaphore_wait(hello, 1)

    pupil_core(0).start()
    for d in range(1, NY):
        pupil_y(d).wait_recv()
        pupil_core(NY - d).start()

    def reduce_x(t, d):
        to = lax.rem(x + d, NX)
        rows = send_x.at[t, pl.ds(pl.multiple_of(to * 128, 128), 128), :]
        return remote(rows, recv_x.at[t, d - 1], rxs_sem.at[t, d - 1], rxr_sem.at[t, d - 1], at_x(d))

    def z_block(d):
        return lax.rem(z + d, NZ) * 16

    def reduce_z(t, d):
        rows = send_z.at[t, pl.ds(pl.multiple_of(z_block(d), 16), 16), :]
        return remote(rows, recv_z.at[t, d - 1], rzs_sem.at[t, d - 1], rzr_sem.at[t, d - 1], at_z(d))

    def turn_x(t):
        for d in range(1, NX):
            reduce_x(t, d).wait_recv()
        for d in FAR_FIRST + (0,):
            rows = pl.ds(pl.multiple_of(z_block(d), 16), 16)
            total = send_x[t, pl.ds(pl.multiple_of(x * 128 + z_block(d), 16), 16), :].astype(F32)
            for w in range(NX - 1):
                total += recv_x[t, w, rows, :].astype(F32)
            send_z[t, rows, :] = total.astype(BF)
            if d:
                reduce_z(t, d).start()

    def turn_z(t):
        total = send_z[t, pl.ds(pl.multiple_of(z * 16, 16), 16), :].astype(F32)
        for d in range(1, NZ):
            reduce_z(t, d).wait_recv()
        for d in range(1, NZ):
            total += recv_z[t, d - 1].astype(F32)
        out[t] = total

    def sums(n, first, t):
        grads = source_block(
            n, GROUPS[n], e[pl.ds(pl.multiple_of(first * 8, 256), n * 8), :], spec[t].reshape(512, 256),
            pupil[pl.ds(pl.multiple_of(first * 32, 1024), n * 32), :],
            right[...], left[...], left_t[...], right_t[...], cot[t],
        )
        weights = et[:, pl.ds(pl.multiple_of(first * 8, 256), n * 8)]
        return [dot(weights, g) for g in grads]

    for d in range(1, NX):
        gather_x(0, d).wait_recv()

    def first_tile(k, carry):
        @pl.when(k == 1)
        def _():
            forward(3)
            for j in range(NY):
                pupil_core(j).wait_recv()

        added = sums(32, lax.rem(core + k, 2) * 32, 0)
        for i in range(NX):
            rows = pl.ds(i * 128, 128)
            acc[rows, :] = acc[rows, :] * k.astype(F32) + added[i]
        return carry

    acc[...] = jnp.zeros_like(acc)
    lax.fori_loop(0, 2, first_tile, 0)
    send_x[0] = acc[...].astype(BF)
    for d in (2, 1, 3):
        reduce_x(0, d).start()

    def one_tile(t, carry):
        @pl.when(t == 1)
        def _():
            for d in range(1, NX):
                gather_x(t, d).wait_recv()

        @pl.when(t > 1)
        def _():
            for d in range(1, NZ):
                then_z(t, d).wait_recv()

        added = sums(64, 0, t)
        for i in range(NX):
            send_x[t, i * 128 : i * 128 + 128, :] = added[i].astype(BF)
        for d in (2, 1, 3):
            reduce_x(t, d).start()

        @pl.when(t == 2)
        def _():
            turn_x(0)

        return carry

    lax.fori_loop(1, 4, one_tile, 0)
    turn_x(1)
    turn_x(2)
    turn_z(0)
    turn_x(3)
    turn_z(1)
    turn_z(2)
    for t in range(4):
        for d in range(1, NZ):
            (then_z if t in (2, 3) else gather_z)(t, d).wait_send()
            if t < 3:
                reduce_z(t, d).wait_send()
        for d in range(1, NX):
            (first_x if t in (2, 3) else gather_x)(t, d).wait_send()
            reduce_x(t, d).wait_send()
    for d in range(1, NY):
        pupil_y(d).wait_send()
    for j in range(NY):
        pupil_core(j).wait_send()
    turn_z(3)
    for d in range(1, NZ):
        reduce_z(3, d).wait_send()


def shards(spectra, cotangent, pupil_field, source_grid, cutoff, stencil, interp_weights, source_weight):
    own_spec = spectra.reshape(4, 8, 2, 2, 128).transpose(0, 1, 3, 2, 4).reshape(64, 2, 128)
    own_pupil = pupil_field.reshape(8, 2, 32, 128).transpose(0, 2, 1, 3).reshape(256, 2, 128)
    vmem = pl.BlockSpec(memory_space=pltpu.VMEM)
    hbm = pl.BlockSpec(memory_space=pl.ANY)
    dma = pltpu.SemaphoreType.DMA
    result = pl.pallas_call(
        kernel,
        out_shape=pltpu.VMEM((4, 16, 256), F32),
        in_specs=[hbm] * 12,
        out_specs=vmem,
        scratch_shapes=[
            pltpu.VMEM((64, 2, 128), BF),
            pltpu.VMEM((256, 2, 128), BF),
            pltpu.VMEM((4, 128, 128), F32),
            pltpu.VMEM((4, 64), jnp.int32),
            pltpu.VMEM((4, 64), BF),
            pltpu.VMEM((1, 64), F32),
            pltpu.SMEM((2, 64), jnp.int32),
            pltpu.SMEM((64,), jnp.int32),
            pltpu.VMEM((256, 512), BF),
            pltpu.VMEM((256, 128), BF),
            pltpu.VMEM((128, 256), BF),
            pltpu.VMEM((512, 256), BF),
            pltpu.VMEM((4, 16, 256), BF),
            pltpu.VMEM((4, NX, 128, 256), BF),
            pltpu.VMEM((2048, 256), BF),
            pltpu.VMEM((512, 128), BF),
            pltpu.VMEM((128, 512), BF),
            pltpu.VMEM((512, 256), F32),
            pltpu.VMEM((4, 512, 256), BF),
            pltpu.VMEM((4, 3, 128, 256), BF),
            pltpu.VMEM((4, 128, 256), BF),
            pltpu.VMEM((4, 7, 16, 256), BF),
            dma((12,)), pltpu.SemaphoreType.REGULAR,
            dma((4, 7)), dma((4, 7)), dma((4, 3)), dma((4, 3)),
            dma((3,)), dma((3,)), dma((4,)), dma((4,)),
            dma((4, 3)), dma((4, 3)), dma((4, 7)), dma((4, 7)),
        ],
        compiler_params=pltpu.CompilerParams(
            collective_id=0, has_side_effects=True, vmem_limit_bytes=56 << 20
        ),
    )(
        own_spec, own_pupil, cotangent, stencil.T, interp_weights.T, source_weight.reshape(1, 64), source_grid.T, cutoff,
        *[jnp.asarray(v) for v in dft_matrices()],
    )
    return result.reshape(4, 8, 2, 2, 128).transpose(0, 1, 3, 2, 4).reshape(4, 8, 2, 256)


def solution(mesh):
    placed = (
        P("tile", "angle", None, "src"),
        P("tile", None, None),
        P(("angle", "src", "tile"), None, None),
        P(("angle", "src"), None),
        P(("angle", "src")),
        P(("angle", "src"), None),
        P(("angle", "src"), None),
        P(("angle", "src")),
    )
    return jax.shard_map(
        shards, mesh=mesh, in_specs=placed, out_specs=P("tile", "angle", None, "src"), check_vma=False
    )
```

```python
import functools
import math

import jax
import jax.numpy as jnp
import ml_dtypes
import numpy as np
from jax import lax
from jax.experimental import pallas as pl
from jax.experimental.pallas import tpu as pltpu
from jax.sharding import PartitionSpec as P

FQ = 64
NP = 128
NX, NY, NZ = 4, 4, 8
BF = jnp.bfloat16
F32 = jnp.float32
MESH = pl.DeviceIdType.MESH
FAR_FIRST = (4, 3, 5, 2, 6, 1, 7)
GROUPS = {32: 4, 64: 8}


def dft_matrices():
    f = np.arange(FQ) - FQ // 2
    phase = np.mod(np.arange(NP)[:, None] * f[None, :], NP) * (2 * math.pi / NP)
    c, s = np.cos(phase) / math.sqrt(FQ), np.sin(phase) / math.sqrt(FQ)
    right = np.zeros((2, 2, 64, 2, 2, 128))
    left = np.zeros((2, 128, 2, 2, 32))
    for p in range(2):
        right[0, p, :, p, 0], right[0, p, :, p, 1] = c.T, s.T
        right[1, p, :, p, 0], right[1, p, :, p, 1] = -s.T, c.T
        left[0, :, p, 0], left[0, :, p, 1] = c[:, p::2], -s[:, p::2]
        left[1, :, p, 0], left[1, :, p, 1] = s[:, p::2], c[:, p::2]
    right, left = right.reshape(256, 512), left.reshape(256, 128)
    return [np.ascontiguousarray(v).astype(ml_dtypes.bfloat16) for v in (right, left, left.T, right.T)]


def dot(a, b):
    return jnp.dot(a, b, preferred_element_type=F32)


def join(values, axis):
    return jnp.concatenate(values, axis=axis)


def source_block(n, h, e, spec, pupil, right, left, left_t, right_t, cot):
    m = n // h
    mixed = [dot(e, spec[x * 128 : x * 128 + 128]) for x in range(NX)]
    pupils, halves = [], []
    for g in range(h):
        p = pupil[g * m * 32 : (g + 1) * m * 32]
        pr, pi = p[:, :128].astype(F32), p[:, 128:].astype(F32)
        pupils.append((pr, pi))
        own = join([mixed[x][s * 8 : s * 8 + 8] for s in range(g * m, (g + 1) * m) for x in range(NX)], 0)
        mr, mi = own[:, :128], own[:, 128:]
        halves.append(join([(pr * mr - pi * mi).astype(BF), (pr * mi + pi * mr).astype(BF)], 1))
    halves = [dot(field, right).astype(BF) for field in halves]
    wide = join([cot, cot], 1)
    wide = join([wide, wide], 0)
    adjoints = []
    for q in range(n // 2):
        pair = []
        for s in (2 * q, 2 * q + 1):
            half, row = halves[s // m], s % m * 32
            pair.append(join([half[row : row + 32, c * 128 : c * 128 + 128] for c in range(4)], 0))
        adjoints.append((dot(left, join(pair, 1)) * wide).astype(BF))
    backs = [dot(left_t, adjoint).astype(BF) for adjoint in adjoints]
    rows = []
    for back in backs:
        for s in range(2):
            rows.append(join([back[c * 32 : c * 32 + 32, s * 128 : s * 128 + 128] for c in range(4)], 1))
    spectra = [dot(join(rows[g * m : (g + 1) * m], 0), right_t) for g in range(h)]
    grads = []
    for (pr, pi), spectrum in zip(pupils, spectra):
        br, bi = spectrum[:, :128], spectrum[:, 128:]
        grads.append(join([pr * br + pi * bi, pr * bi - pi * br], 1))
    return [
        join([grads[s // m][s % m * 32 + x * 8 : s % m * 32 + x * 8 + 8] for s in range(n)], 0).astype(BF)
        for x in range(NX)
    ]


def kernel(
    spec_hbm, pupil_hbm, cot_hbm, stencil_hbm, interp_hbm, weight_hbm, grid_hbm, cutoff_hbm,
    right_hbm, left_hbm, left_t_hbm, right_t_hbm,
    out,
    raw_spec, raw_pupil, cot, stencil, interp, weight, grid, cutoff, right, left, left_t, right_t,
    own_spec, spec, pupil, e, et, acc, send_x, recv_x, send_z, recv_z, recv_far,
    in_sem, hello, zs_sem, zr_sem, xs_sem, xr_sem, ps_sem, pr_sem, cs_sem, cr_sem, rxs_sem, rxr_sem, rzs_sem, rzr_sem, far_s_sem, far_r_sem,
):
    angle, src, tile = lax.axis_index("angle"), lax.axis_index("src"), lax.axis_index("tile")
    x, z = src // 4, angle * 4 + lax.rem(src, 4)
    y, core = tile // 2, lax.rem(tile, 2)

    def at_x(d):
        return {"src": lax.rem(x + d, NX) * 4 + lax.rem(src, 4)}

    def at_z(d):
        w = lax.rem(z + d, NZ)
        return {"angle": w // 4, "src": x * 4 + lax.rem(w, 4)}

    def at_y(d):
        return {"tile": lax.rem(y + d, NY) * 2 + core}

    twin = {"tile": y * 2 + 1 - core}
    peers = [at_z(d) for d in FAR_FIRST] + [at_x(d) for d in (2, 1, 3)] + [at_y(d) for d in (2, 1, 3)]
    barrier = pltpu.get_barrier_semaphore()
    for peer in peers:
        pl.semaphore_signal(barrier, inc=1, device_id=peer, device_id_type=MESH)

    @pl.when(core == 0)
    def _():
        pl.semaphore_signal(barrier, inc=1, device_id=twin, device_id_type=MESH)

    pairs = [
        (spec_hbm, raw_spec), (grid_hbm, grid), (cutoff_hbm, cutoff), (pupil_hbm, raw_pupil), (stencil_hbm, stencil),
        (interp_hbm, interp), (weight_hbm, weight), (right_hbm, right), (left_hbm, left), (cot_hbm, cot),
        (left_t_hbm, left_t), (right_t_hbm, right_t),
    ]
    loads = [pltpu.make_async_copy(a, b, in_sem.at[i]) for i, (a, b) in enumerate(pairs)]
    for load in loads:
        load.start()

    loads[0].wait()
    for t in range(4):
        part = raw_spec[t * 16 : t * 16 + 16]
        own_spec[t] = join([part[:, 0], part[:, 1]], 1)

    for load in loads[1:4]:
        load.wait()
    lane = lax.broadcasted_iota(jnp.int32, (32, 128), 1)
    fa = 2 * lax.broadcasted_iota(jnp.int32, (32, 128), 0) + (lane >> 6) - 32
    fb = (lane & 63) - 32

    def mask(s8, carry):
        s = tile * 8 + s8
        da, db = fa + grid[0, s], fb + grid[1, s]
        inside = da * da + db * db <= cutoff[s]
        inside = join([inside, inside], 1)
        part = raw_pupil[pl.ds(pl.multiple_of(s8 * 32, 32), 32)]
        value = join([part[:, 0], part[:, 1]], 1).astype(F32)
        rows = pl.ds(pl.multiple_of((core * 4 + y) * 256 + s8 * 32, 32), 32)
        pupil[rows, :] = jnp.where(inside, value, 0.0).astype(BF)
        return carry

    lax.fori_loop(0, 8, mask, 0)

    pl.semaphore_wait(barrier, len(peers) + core)

    @pl.when(core == 1)
    def _():
        pl.semaphore_signal(hello, inc=1, device_id=twin, device_id_type=MESH)

    def remote(src_ref, dst_ref, send, recv, peer):
        return pltpu.make_async_remote_copy(
            src_ref=src_ref, dst_ref=dst_ref, send_sem=send, recv_sem=recv, device_id=peer, device_id_type=MESH
        )

    zrows = pl.ds(pl.multiple_of(z * 16, 16), 16)
    xrows = pl.ds(pl.multiple_of(x * 128, 128), 128)

    def gather_z(t, d):
        return remote(own_spec.at[t], spec.at[t, x, zrows, :], zs_sem.at[t, d - 1], zr_sem.at[t, d - 1], at_z(d))

    def gather_x(t, d):
        rows = spec.at[t, x]
        return remote(rows, rows, xs_sem.at[t, d - 1], xr_sem.at[t, d - 1], at_x(d))

    def first_x(t, d):
        return remote(own_spec.at[t], spec.at[t, x, zrows, :], xs_sem.at[t, d - 1], xr_sem.at[t, d - 1], at_x(d))

    def then_z(t, d):
        rows = spec.at[t, :, zrows, :]
        return remote(rows, rows, zs_sem.at[t, d - 1], zr_sem.at[t, d - 1], at_z(d))

    def forward(t):
        for d in range(1, NX):
            first_x(t, d).wait_recv()
        for d in FAR_FIRST:
            then_z(t, d).start()

    def pupil_rows(yy):
        return pl.ds(pl.multiple_of((core * 4 + yy) * 256, 256), 256)

    def pupil_y(d):
        rows = pupil.at[pupil_rows(y), :]
        return remote(rows, rows, ps_sem.at[d - 1], pr_sem.at[d - 1], at_y(d))

    def pupil_core(j):
        rows = pupil.at[pupil_rows(lax.rem(y + j, NY)), :]
        return remote(rows, rows, cs_sem.at[j], cr_sem.at[j], twin)

    for d in FAR_FIRST:
        gather_z(0, d).start()
    for d in (2, 1, 3):
        first_x(2, d).start()
    for d in (2, 1, 3):
        first_x(3, d).start()

    for d in (2, 1, 3):
        pupil_y(d).start()
    for d in FAR_FIRST:
        gather_z(1, d).start()
    for t in range(4):
        spec[t, x, zrows, :] = own_spec[t]

    for load in loads[4:7]:
        load.wait()
    c = lax.broadcasted_iota(jnp.int32, (128, 64), 0)
    k_of = (c >> 6) * 8 + ((c >> 1) & 7)
    mix = jnp.zeros((128, 64), F32)
    for j in range(4):
        mix += jnp.where(stencil[j : j + 1, :] == k_of, interp[j : j + 1, :].astype(F32), 0.0)
    scaled = (mix * (weight[...] * (2.0 / math.sqrt(2048)))).astype(BF)
    mix = mix.astype(BF)
    c = lax.broadcasted_iota(jnp.int32, (128, 256), 0)
    col = lax.broadcasted_iota(jnp.int32, (128, 256), 1)
    hit = (col & 7) == ((c >> 4) & 3) * 2 + (c & 1)
    source_at = lax.broadcasted_iota(jnp.int32, (64, 256), 0)
    col = lax.broadcasted_iota(jnp.int32, (64, 256), 1)
    source_of = (col >> 6) * 16 + ((col >> 3) & 7)
    for k in range(2):
        pick = (source_of + k * 8 == source_at).astype(BF)
        et[:, k * 256 : k * 256 + 256] = jnp.where(hit, dot(scaled, pick), 0.0).astype(BF)
        e[k * 256 : k * 256 + 256, :] = jnp.where(hit, dot(mix, pick), 0.0).T.astype(BF)

    for load in loads[7:]:
        load.wait()

    for d in range(1, NZ):
        gather_z(0, d).wait_recv()
    for d in (2, 1, 3):
        gather_x(0, d).start()

    for d in range(1, NZ):
        gather_z(1, d).wait_recv()
    for d in (2, 1, 3):
        gather_x(1, d).start()

    forward(2)

    @pl.when(core == 0)
    def _():
        pl.semaphore_wait(hello, 1)

    pupil_core(0).start()
    for d in range(1, NY):
        pupil_y(d).wait_recv()
        pupil_core(NY - d).start()

    def reduce_x(t, d):
        to = lax.rem(x + d, NX)
        rows = send_x.at[t, pl.ds(pl.multiple_of(to * 128, 128), 128), :]
        return remote(rows, recv_x.at[t, d - 1], rxs_sem.at[t, d - 1], rxr_sem.at[t, d - 1], at_x(d))

    def z_block(d):
        return lax.rem(z + d, NZ) * 16

    def reduce_z(t, d):
        rows = send_z.at[t, pl.ds(pl.multiple_of(z_block(d), 16), 16), :]
        return remote(rows, recv_z.at[t, d - 1], rzs_sem.at[t, d - 1], rzr_sem.at[t, d - 1], at_z(d))

    def reduce_far(d):
        rows = send_x.at[3, pl.ds(pl.multiple_of(lax.rem(x + 2, NX) * 128 + z_block(d), 16), 16), :]
        w = lax.rem(z + d, NZ)
        peer = {"angle": w // 4, "src": lax.rem(x + 2, NX) * 4 + lax.rem(w, 4)}
        return remote(rows, recv_far.at[d], far_s_sem.at[d], far_r_sem.at[d], peer)

    def turn_x(t):
        steps = (1, 3) if isinstance(t, int) and t == 3 else (1, 2, 3)
        for d in steps:
            reduce_x(t, d).wait_recv()
        for d in FAR_FIRST + (0,):
            rows = pl.ds(pl.multiple_of(z_block(d), 16), 16)
            total = send_x[t, pl.ds(pl.multiple_of(x * 128 + z_block(d), 16), 16), :].astype(F32)
            for w in steps:
                total += recv_x[t, w - 1, rows, :].astype(F32)
            send_z[t, rows, :] = total.astype(BF)
            if d:
                reduce_z(t, d).start()

    def turn_z(t):
        total = send_z[t, pl.ds(pl.multiple_of(z * 16, 16), 16), :].astype(F32)
        for d in range(1, NZ):
            reduce_z(t, d).wait_recv()
        for d in range(1, NZ):
            total += recv_z[t, d - 1].astype(F32)
        if t == 3:
            for d in range(NZ):
                reduce_far(d).wait_recv()
            for d in range(NZ):
                total += recv_far[d].astype(F32)
        out[t] = total

    def sums(n, first, t):
        grads = source_block(
            n, GROUPS[n], e[pl.ds(pl.multiple_of(first * 8, 256), n * 8), :], spec[t].reshape(512, 256),
            pupil[pl.ds(pl.multiple_of(first * 32, 1024), n * 32), :],
            right[...], left[...], left_t[...], right_t[...], cot[t],
        )
        weights = et[:, pl.ds(pl.multiple_of(first * 8, 256), n * 8)]
        return [dot(weights, g) for g in grads]

    for d in range(1, NX):
        gather_x(0, d).wait_recv()

    def first_tile(k, carry):
        @pl.when(k == 1)
        def _():
            forward(3)
            for j in range(NY):
                pupil_core(j).wait_recv()

        added = sums(32, lax.rem(core + k, 2) * 32, 0)
        for i in range(NX):
            rows = pl.ds(i * 128, 128)
            acc[rows, :] = acc[rows, :] * k.astype(F32) + added[i]
        return carry

    acc[...] = jnp.zeros_like(acc)
    lax.fori_loop(0, 2, first_tile, 0)
    send_x[0] = acc[...].astype(BF)
    for d in (2, 1, 3):
        reduce_x(0, d).start()

    def one_tile(t, carry):
        @pl.when(t == 1)
        def _():
            for d in range(1, NX):
                gather_x(t, d).wait_recv()

        @pl.when(t > 1)
        def _():
            for d in range(1, NZ):
                then_z(t, d).wait_recv()

        added = sums(64, 0, t)
        for i in range(NX):
            send_x[t, i * 128 : i * 128 + 128, :] = added[i].astype(BF)
        for d in (1, 3):
            reduce_x(t, d).start()

        @pl.when(t < 3)
        def _():
            reduce_x(t, 2).start()

        @pl.when(t == 3)
        def _():
            for d in FAR_FIRST + (0,):
                reduce_far(d).start()

        @pl.when(t == 2)
        def _():
            turn_x(0)

        return carry

    lax.fori_loop(1, 4, one_tile, 0)
    turn_x(1)
    turn_x(2)
    turn_z(0)
    turn_x(3)
    turn_z(1)
    turn_z(2)
    for t in range(4):
        for d in range(1, NZ):
            (then_z if t in (2, 3) else gather_z)(t, d).wait_send()
            if t < 3:
                reduce_z(t, d).wait_send()
        for d in range(1, NX):
            (first_x if t in (2, 3) else gather_x)(t, d).wait_send()
            if t < 3 or d != 2:
                reduce_x(t, d).wait_send()
    for d in range(1, NY):
        pupil_y(d).wait_send()
    for j in range(NY):
        pupil_core(j).wait_send()
    for d in range(NZ):
        reduce_far(d).wait_send()
    turn_z(3)
    for d in range(1, NZ):
        reduce_z(3, d).wait_send()


def shards(spectra, cotangent, pupil_field, source_grid, cutoff, stencil, interp_weights, source_weight):
    own_spec = spectra.reshape(4, 8, 2, 2, 128).transpose(0, 1, 3, 2, 4).reshape(64, 2, 128)
    own_pupil = pupil_field.reshape(8, 2, 32, 128).transpose(0, 2, 1, 3).reshape(256, 2, 128)
    vmem = pl.BlockSpec(memory_space=pltpu.VMEM)
    hbm = pl.BlockSpec(memory_space=pl.ANY)
    dma = pltpu.SemaphoreType.DMA
    result = pl.pallas_call(
        kernel,
        out_shape=pltpu.VMEM((4, 16, 256), F32),
        in_specs=[hbm] * 12,
        out_specs=vmem,
        scratch_shapes=[
            pltpu.VMEM((64, 2, 128), BF),
            pltpu.VMEM((256, 2, 128), BF),
            pltpu.VMEM((4, 128, 128), F32),
            pltpu.VMEM((4, 64), jnp.int32),
            pltpu.VMEM((4, 64), BF),
            pltpu.VMEM((1, 64), F32),
            pltpu.SMEM((2, 64), jnp.int32),
            pltpu.SMEM((64,), jnp.int32),
            pltpu.VMEM((256, 512), BF),
            pltpu.VMEM((256, 128), BF),
            pltpu.VMEM((128, 256), BF),
            pltpu.VMEM((512, 256), BF),
            pltpu.VMEM((4, 16, 256), BF),
            pltpu.VMEM((4, NX, 128, 256), BF),
            pltpu.VMEM((2048, 256), BF),
            pltpu.VMEM((512, 128), BF),
            pltpu.VMEM((128, 512), BF),
            pltpu.VMEM((512, 256), F32),
            pltpu.VMEM((4, 512, 256), BF),
            pltpu.VMEM((4, 3, 128, 256), BF),
            pltpu.VMEM((4, 128, 256), BF),
            pltpu.VMEM((4, 7, 16, 256), BF),
            pltpu.VMEM((8, 16, 256), BF),
            dma((12,)), pltpu.SemaphoreType.REGULAR,
            dma((4, 7)), dma((4, 7)), dma((4, 3)), dma((4, 3)),
            dma((3,)), dma((3,)), dma((4,)), dma((4,)),
            dma((4, 3)), dma((4, 3)), dma((4, 7)), dma((4, 7)), dma((8,)), dma((8,)),
        ],
        compiler_params=pltpu.CompilerParams(
            collective_id=0, has_side_effects=True, vmem_limit_bytes=56 << 20
        ),
    )(
        own_spec, own_pupil, cotangent, stencil.T, interp_weights.T, source_weight.reshape(1, 64), source_grid.T, cutoff,
        *[jnp.asarray(v) for v in dft_matrices()],
    )
    return result.reshape(4, 8, 2, 2, 128).transpose(0, 1, 3, 2, 4).reshape(4, 8, 2, 256)


def solution(mesh):
    placed = (
        P("tile", "angle", None, "src"),
        P("tile", None, None),
        P(("angle", "src", "tile"), None, None),
        P(("angle", "src"), None),
        P(("angle", "src")),
        P(("angle", "src"), None),
        P(("angle", "src"), None),
        P(("angle", "src")),
    )
    return jax.shard_map(
        shards, mesh=mesh, in_specs=placed, out_specs=P("tile", "angle", None, "src"), check_vma=False
    )
```

```python
import functools
import math

import jax
import jax.numpy as jnp
import ml_dtypes
import numpy as np
from jax import lax
from jax.experimental import pallas as pl
from jax.experimental.pallas import tpu as pltpu
from jax.sharding import PartitionSpec as P

FQ = 64
NP = 128
NX, NY, NZ = 4, 4, 8
BF = jnp.bfloat16
F32 = jnp.float32
MESH = pl.DeviceIdType.MESH
FAR_FIRST = (4, 3, 5, 2, 6, 1, 7)
GROUPS = {32: 4, 64: 8}


def dft_matrices():
    f = np.arange(FQ) - FQ // 2
    phase = np.mod(np.arange(NP)[:, None] * f[None, :], NP) * (2 * math.pi / NP)
    c, s = np.cos(phase) / math.sqrt(FQ), np.sin(phase) / math.sqrt(FQ)
    right = np.zeros((2, 2, 64, 2, 2, 128))
    left = np.zeros((2, 128, 2, 2, 32))
    for p in range(2):
        right[0, p, :, p, 0], right[0, p, :, p, 1] = c.T, s.T
        right[1, p, :, p, 0], right[1, p, :, p, 1] = -s.T, c.T
        left[0, :, p, 0], left[0, :, p, 1] = c[:, p::2], -s[:, p::2]
        left[1, :, p, 0], left[1, :, p, 1] = s[:, p::2], c[:, p::2]
    right, left = right.reshape(256, 512), left.reshape(256, 128)
    return [np.ascontiguousarray(v).astype(ml_dtypes.bfloat16) for v in (right, left, left.T, right.T)]


def dot(a, b):
    return jnp.dot(a, b, preferred_element_type=F32)


def join(values, axis):
    return jnp.concatenate(values, axis=axis)


def source_block(n, h, e, spec, pupil, right, left, left_t, right_t, cot):
    m = n // h
    mixed = [dot(e, spec[x * 128 : x * 128 + 128]) for x in range(NX)]
    pupils, halves = [], []
    for g in range(h):
        p = pupil[g * m * 32 : (g + 1) * m * 32]
        pr, pi = p[:, :128].astype(F32), p[:, 128:].astype(F32)
        pupils.append((pr, pi))
        own = join([mixed[x][s * 8 : s * 8 + 8] for s in range(g * m, (g + 1) * m) for x in range(NX)], 0)
        mr, mi = own[:, :128], own[:, 128:]
        halves.append(join([(pr * mr - pi * mi).astype(BF), (pr * mi + pi * mr).astype(BF)], 1))
    halves = [dot(field, right).astype(BF) for field in halves]
    wide = join([cot, cot], 1)
    wide = join([wide, wide], 0)
    adjoints = []
    for q in range(n // 2):
        pair = []
        for s in (2 * q, 2 * q + 1):
            half, row = halves[s // m], s % m * 32
            pair.append(join([half[row : row + 32, c * 128 : c * 128 + 128] for c in range(4)], 0))
        adjoints.append((dot(left, join(pair, 1)) * wide).astype(BF))
    backs = [dot(left_t, adjoint).astype(BF) for adjoint in adjoints]
    rows = []
    for back in backs:
        for s in range(2):
            rows.append(join([back[c * 32 : c * 32 + 32, s * 128 : s * 128 + 128] for c in range(4)], 1))
    spectra = [dot(join(rows[g * m : (g + 1) * m], 0), right_t) for g in range(h)]
    grads = []
    for (pr, pi), spectrum in zip(pupils, spectra):
        br, bi = spectrum[:, :128], spectrum[:, 128:]
        grads.append(join([pr * br + pi * bi, pr * bi - pi * br], 1))
    return [
        join([grads[s // m][s % m * 32 + x * 8 : s % m * 32 + x * 8 + 8] for s in range(n)], 0).astype(BF)
        for x in range(NX)
    ]


def kernel(
    spec_hbm, pupil_hbm, cot_hbm, stencil_hbm, interp_hbm, weight_hbm, grid_hbm, cutoff_hbm,
    right_hbm, left_hbm, left_t_hbm, right_t_hbm,
    out,
    raw_spec, raw_pupil, cot, stencil, interp, weight, grid, cutoff, right, left, left_t, right_t,
    own_spec, spec, pupil, e, et, acc, send_x, recv_x, send_z, recv_z, recv_far,
    in_sem, hello, zs_sem, zr_sem, xs_sem, xr_sem, ps_sem, pr_sem, cs_sem, cr_sem, rxs_sem, rxr_sem, rzs_sem, rzr_sem, far_s_sem, far_r_sem,
):
    angle, src, tile = lax.axis_index("angle"), lax.axis_index("src"), lax.axis_index("tile")
    x, z = src // 4, angle * 4 + lax.rem(src, 4)
    y, core = tile // 2, lax.rem(tile, 2)

    def at_x(d):
        return {"src": lax.rem(x + d, NX) * 4 + lax.rem(src, 4)}

    def at_z(d):
        w = lax.rem(z + d, NZ)
        return {"angle": w // 4, "src": x * 4 + lax.rem(w, 4)}

    def at_y(d):
        return {"tile": lax.rem(y + d, NY) * 2 + core}

    twin = {"tile": y * 2 + 1 - core}
    peers = [at_z(d) for d in FAR_FIRST] + [at_x(d) for d in (2, 1, 3)] + [at_y(d) for d in (2, 1, 3)]
    barrier = pltpu.get_barrier_semaphore()
    for peer in peers:
        pl.semaphore_signal(barrier, inc=1, device_id=peer, device_id_type=MESH)

    @pl.when(core == 0)
    def _():
        pl.semaphore_signal(barrier, inc=1, device_id=twin, device_id_type=MESH)

    pairs = [
        (spec_hbm, raw_spec), (grid_hbm, grid), (cutoff_hbm, cutoff), (pupil_hbm, raw_pupil), (stencil_hbm, stencil),
        (interp_hbm, interp), (weight_hbm, weight), (right_hbm, right), (left_hbm, left), (cot_hbm, cot),
        (left_t_hbm, left_t), (right_t_hbm, right_t),
    ]
    loads = [pltpu.make_async_copy(a, b, in_sem.at[i]) for i, (a, b) in enumerate(pairs)]
    for load in loads:
        load.start()

    loads[0].wait()
    for t in range(4):
        part = raw_spec[t * 16 : t * 16 + 16]
        own_spec[t] = join([part[:, 0], part[:, 1]], 1)

    for load in loads[1:4]:
        load.wait()
    lane = lax.broadcasted_iota(jnp.int32, (32, 128), 1)
    fa = 2 * lax.broadcasted_iota(jnp.int32, (32, 128), 0) + (lane >> 6) - 32
    fb = (lane & 63) - 32

    def mask(s8, carry):
        s = tile * 8 + s8
        da, db = fa + grid[0, s], fb + grid[1, s]
        inside = da * da + db * db <= cutoff[s]
        inside = join([inside, inside], 1)
        part = raw_pupil[pl.ds(pl.multiple_of(s8 * 32, 32), 32)]
        value = join([part[:, 0], part[:, 1]], 1).astype(F32)
        rows = pl.ds(pl.multiple_of((core * 4 + y) * 256 + s8 * 32, 32), 32)
        pupil[rows, :] = jnp.where(inside, value, 0.0).astype(BF)
        return carry

    lax.fori_loop(0, 8, mask, 0)

    pl.semaphore_wait(barrier, len(peers) + core)

    @pl.when(core == 1)
    def _():
        pl.semaphore_signal(hello, inc=1, device_id=twin, device_id_type=MESH)

    def remote(src_ref, dst_ref, send, recv, peer):
        return pltpu.make_async_remote_copy(
            src_ref=src_ref, dst_ref=dst_ref, send_sem=send, recv_sem=recv, device_id=peer, device_id_type=MESH
        )

    zrows = pl.ds(pl.multiple_of(z * 16, 16), 16)
    xrows = pl.ds(pl.multiple_of(x * 128, 128), 128)

    def gather_z(t, d):
        return remote(own_spec.at[t], spec.at[t, x, zrows, :], zs_sem.at[t, d - 1], zr_sem.at[t, d - 1], at_z(d))

    def gather_x(t, d):
        rows = spec.at[t, x]
        return remote(rows, rows, xs_sem.at[t, d - 1], xr_sem.at[t, d - 1], at_x(d))

    def first_x(t, d):
        return remote(own_spec.at[t], spec.at[t, x, zrows, :], xs_sem.at[t, d - 1], xr_sem.at[t, d - 1], at_x(d))

    def then_z(t, d):
        rows = spec.at[t, :, zrows, :]
        return remote(rows, rows, zs_sem.at[t, d - 1], zr_sem.at[t, d - 1], at_z(d))

    def forward(t):
        for d in range(1, NX):
            first_x(t, d).wait_recv()
        for d in FAR_FIRST:
            then_z(t, d).start()

    def pupil_rows(yy):
        return pl.ds(pl.multiple_of((core * 4 + yy) * 256, 256), 256)

    def pupil_y(d):
        rows = pupil.at[pupil_rows(y), :]
        return remote(rows, rows, ps_sem.at[d - 1], pr_sem.at[d - 1], at_y(d))

    def pupil_core(j):
        rows = pupil.at[pupil_rows(lax.rem(y + j, NY)), :]
        return remote(rows, rows, cs_sem.at[j], cr_sem.at[j], twin)

    for d in FAR_FIRST:
        gather_z(0, d).start()
    for d in (2, 1, 3):
        first_x(2, d).start()
    for d in (2, 1, 3):
        first_x(3, d).start()

    for d in (2, 1, 3):
        pupil_y(d).start()
    for d in FAR_FIRST:
        gather_z(1, d).start()
    for t in range(4):
        spec[t, x, zrows, :] = own_spec[t]

    for load in loads[4:7]:
        load.wait()
    c = lax.broadcasted_iota(jnp.int32, (128, 64), 0)
    k_of = (c >> 6) * 8 + ((c >> 1) & 7)
    mix = jnp.zeros((128, 64), F32)
    for j in range(4):
        mix += jnp.where(stencil[j : j + 1, :] == k_of, interp[j : j + 1, :].astype(F32), 0.0)
    scaled = (mix * (weight[...] * (2.0 / math.sqrt(2048)))).astype(BF)
    mix = mix.astype(BF)
    c = lax.broadcasted_iota(jnp.int32, (128, 256), 0)
    col = lax.broadcasted_iota(jnp.int32, (128, 256), 1)
    hit = (col & 7) == ((c >> 4) & 3) * 2 + (c & 1)
    source_at = lax.broadcasted_iota(jnp.int32, (64, 256), 0)
    col = lax.broadcasted_iota(jnp.int32, (64, 256), 1)
    source_of = (col >> 6) * 16 + ((col >> 3) & 7)
    for k in range(2):
        pick = (source_of + k * 8 == source_at).astype(BF)
        et[:, k * 256 : k * 256 + 256] = jnp.where(hit, dot(scaled, pick), 0.0).astype(BF)
        e[k * 256 : k * 256 + 256, :] = jnp.where(hit, dot(mix, pick), 0.0).T.astype(BF)

    for load in loads[7:]:
        load.wait()

    for d in range(1, NZ):
        gather_z(0, d).wait_recv()
    for d in (2, 1, 3):
        gather_x(0, d).start()

    for d in range(1, NZ):
        gather_z(1, d).wait_recv()
    for d in (2, 1, 3):
        gather_x(1, d).start()

    forward(2)

    @pl.when(core == 0)
    def _():
        pl.semaphore_wait(hello, 1)

    pupil_core(0).start()
    for d in range(1, NY):
        pupil_y(d).wait_recv()
        pupil_core(NY - d).start()

    def reduce_x(t, d):
        to = lax.rem(x + d, NX)
        rows = send_x.at[t, pl.ds(pl.multiple_of(to * 128, 128), 128), :]
        return remote(rows, recv_x.at[t, d - 1], rxs_sem.at[t, d - 1], rxr_sem.at[t, d - 1], at_x(d))

    def z_block(d):
        return lax.rem(z + d, NZ) * 16

    def reduce_z(t, d):
        rows = send_z.at[t, pl.ds(pl.multiple_of(z_block(d), 16), 16), :]
        return remote(rows, recv_z.at[t, d - 1], rzs_sem.at[t, d - 1], rzr_sem.at[t, d - 1], at_z(d))

    def reduce_far(d):
        rows = send_x.at[3, pl.ds(pl.multiple_of(lax.rem(x + 2, NX) * 128 + z_block(d), 16), 16), :]
        w = lax.rem(z + d, NZ)
        peer = {"angle": w // 4, "src": lax.rem(x + 2, NX) * 4 + lax.rem(w, 4)}
        return remote(rows, recv_far.at[d], far_s_sem.at[d], far_r_sem.at[d], peer)

    def turn_x(t):
        steps = (1, 3) if isinstance(t, int) and t == 3 else (1, 2, 3)
        for d in steps:
            reduce_x(t, d).wait_recv()
        for d in FAR_FIRST + (0,):
            rows = pl.ds(pl.multiple_of(z_block(d), 16), 16)
            total = send_x[t, pl.ds(pl.multiple_of(x * 128 + z_block(d), 16), 16), :].astype(F32)
            for w in steps:
                total += recv_x[t, w - 1, rows, :].astype(F32)
            send_z[t, rows, :] = total.astype(BF)
            if d:
                reduce_z(t, d).start()

    def turn_z(t):
        total = send_z[t, pl.ds(pl.multiple_of(z * 16, 16), 16), :].astype(F32)
        if t == 3:
            for d in range(NZ):
                reduce_far(d).wait_recv()
            for d in range(NZ):
                total += recv_far[d].astype(F32)
        for d in range(1, NZ):
            reduce_z(t, d).wait_recv()
        for d in range(1, NZ):
            total += recv_z[t, d - 1].astype(F32)
        out[t] = total

    def sums(n, first, t):
        grads = source_block(
            n, GROUPS[n], e[pl.ds(pl.multiple_of(first * 8, 256), n * 8), :], spec[t].reshape(512, 256),
            pupil[pl.ds(pl.multiple_of(first * 32, 1024), n * 32), :],
            right[...], left[...], left_t[...], right_t[...], cot[t],
        )
        weights = et[:, pl.ds(pl.multiple_of(first * 8, 256), n * 8)]
        return [dot(weights, g) for g in grads]

    acc[...] = jnp.zeros_like(acc)
    for d in range(1, NX):
        gather_x(0, d).wait_recv()

    def first_tile(k, carry):
        @pl.when(k == 1)
        def _():
            forward(3)
            for j in range(NY):
                pupil_core(j).wait_recv()

        added = sums(32, lax.rem(core + k, 2) * 32, 0)
        for i in range(NX):
            rows = pl.ds(i * 128, 128)
            acc[rows, :] = acc[rows, :] * k.astype(F32) + added[i]
        return carry

    lax.fori_loop(0, 2, first_tile, 0)
    send_x[0] = acc[...].astype(BF)
    for d in (2, 1, 3):
        reduce_x(0, d).start()

    def one_tile(t, carry):
        @pl.when(t == 1)
        def _():
            for d in range(1, NX):
                gather_x(t, d).wait_recv()

        @pl.when(t > 1)
        def _():
            for d in range(1, NZ):
                then_z(t, d).wait_recv()

        added = sums(64, 0, t)
        for i in range(NX):
            send_x[t, i * 128 : i * 128 + 128, :] = added[i].astype(BF)
        for d in (1, 3):
            reduce_x(t, d).start()

        @pl.when(t < 3)
        def _():
            reduce_x(t, 2).start()

        @pl.when(t == 3)
        def _():
            for d in FAR_FIRST + (0,):
                reduce_far(d).start()

        @pl.when(t == 2)
        def _():
            turn_x(0)

        return carry

    lax.fori_loop(1, 4, one_tile, 0)
    turn_x(1)
    turn_x(2)
    turn_z(0)
    turn_x(3)
    turn_z(1)
    turn_z(2)
    for t in range(4):
        for d in range(1, NZ):
            (then_z if t in (2, 3) else gather_z)(t, d).wait_send()
            if t < 3:
                reduce_z(t, d).wait_send()
        for d in range(1, NX):
            (first_x if t in (2, 3) else gather_x)(t, d).wait_send()
            if t < 3 or d != 2:
                reduce_x(t, d).wait_send()
    for d in range(1, NY):
        pupil_y(d).wait_send()
    for j in range(NY):
        pupil_core(j).wait_send()
    for d in range(NZ):
        reduce_far(d).wait_send()
    turn_z(3)
    for d in range(1, NZ):
        reduce_z(3, d).wait_send()


def shards(spectra, cotangent, pupil_field, source_grid, cutoff, stencil, interp_weights, source_weight):
    own_spec = spectra.reshape(4, 8, 2, 2, 128).transpose(0, 1, 3, 2, 4).reshape(64, 2, 128)
    own_pupil = pupil_field.reshape(8, 2, 32, 128).transpose(0, 2, 1, 3).reshape(256, 2, 128)
    vmem = pl.BlockSpec(memory_space=pltpu.VMEM)
    hbm = pl.BlockSpec(memory_space=pl.ANY)
    dma = pltpu.SemaphoreType.DMA
    result = pl.pallas_call(
        kernel,
        out_shape=pltpu.VMEM((4, 16, 256), F32),
        in_specs=[hbm] * 12,
        out_specs=vmem,
        scratch_shapes=[
            pltpu.VMEM((64, 2, 128), BF),
            pltpu.VMEM((256, 2, 128), BF),
            pltpu.VMEM((4, 128, 128), F32),
            pltpu.VMEM((4, 64), jnp.int32),
            pltpu.VMEM((4, 64), BF),
            pltpu.VMEM((1, 64), F32),
            pltpu.SMEM((2, 64), jnp.int32),
            pltpu.SMEM((64,), jnp.int32),
            pltpu.VMEM((256, 512), BF),
            pltpu.VMEM((256, 128), BF),
            pltpu.VMEM((128, 256), BF),
            pltpu.VMEM((512, 256), BF),
            pltpu.VMEM((4, 16, 256), BF),
            pltpu.VMEM((4, NX, 128, 256), BF),
            pltpu.VMEM((2048, 256), BF),
            pltpu.VMEM((512, 128), BF),
            pltpu.VMEM((128, 512), BF),
            pltpu.VMEM((512, 256), F32),
            pltpu.VMEM((4, 512, 256), BF),
            pltpu.VMEM((4, 3, 128, 256), BF),
            pltpu.VMEM((4, 128, 256), BF),
            pltpu.VMEM((4, 7, 16, 256), BF),
            pltpu.VMEM((8, 16, 256), BF),
            dma((12,)), pltpu.SemaphoreType.REGULAR,
            dma((4, 7)), dma((4, 7)), dma((4, 3)), dma((4, 3)),
            dma((3,)), dma((3,)), dma((4,)), dma((4,)),
            dma((4, 3)), dma((4, 3)), dma((4, 7)), dma((4, 7)), dma((8,)), dma((8,)),
        ],
        compiler_params=pltpu.CompilerParams(
            collective_id=0, has_side_effects=True, vmem_limit_bytes=56 << 20
        ),
    )(
        own_spec, own_pupil, cotangent, stencil.T, interp_weights.T, source_weight.reshape(1, 64), source_grid.T, cutoff,
        *[jnp.asarray(v) for v in dft_matrices()],
    )
    return result.reshape(4, 8, 2, 2, 128).transpose(0, 1, 3, 2, 4).reshape(4, 8, 2, 256)


def solution(mesh):
    placed = (
        P("tile", "angle", None, "src"),
        P("tile", None, None),
        P(("angle", "src", "tile"), None, None),
        P(("angle", "src"), None),
        P(("angle", "src")),
        P(("angle", "src"), None),
        P(("angle", "src"), None),
        P(("angle", "src")),
    )
    return jax.shard_map(
        shards, mesh=mesh, in_specs=placed, out_specs=P("tile", "angle", None, "src"), check_vma=False
    )
```
